128 devices in a mesh: brick: 32 (over z, y, core), ana: 4 (over x).
Axes of the slice: x: 4, y: 4, z: 4, core: 2. Of those that a mesh axis runs over, the one named last changes fastest.
Arguments:
- provisional: float32 [4, 3, 512, 128, 256], P(None, None, 'brick', 'ana'), may hold values from -120 to 120
- sample_index: int32 [32, 4, 32768], P('brick', 'ana'), may hold values from 0 to 131071, as said below
- owner_table: int32 [32, 32], replicated, may hold values from 0 to 31, each once within a row
- weighted_basis: float32 [16, 3, 4194304], P(None, None, ('brick', 'ana')), may hold values from -200 to 200
Outputs:
- new_basis: float32 [20, 3, 4194304], P(None, None, ('brick', 'ana'))
- core_factor: float32 [20, 20], replicated
The draws below stay inside these ranges and needn't reach their ends.
Inputs may be any that keep to these rules, and one draw needn't show every extreme that they name: sample_index[b, a, j] lies between 4 j and 4 j + 3. `owner_table`: each row names every brick index once.
All inputs are finite; a program needn't handle non-finite values.
Results may differ from the reference program's by a relative error of at most 0.00021.
Values sent between devices are 32-bit elements; how exact they have to be, the bound alone decides.
No kernel may reach another device: no remote copies, remote signals or barrier semaphores. Data moves between devices by JAX's collectives and lax.ppermute only.
A program may use at most 128 MiB of HBM per device.

```python
import jax
import jax.numpy as jnp
from jax import lax

CX = 16
CY = 32
CZ = 256
NSNAP = 4
RANK = 16
NX = 512
NY = 128
SAMP_DEV = 32768
SBLK = 1024
ROWS = 4194304
N_BRICK = 32
N_ANA = 4


def draw_provisional(key, part):
    key = jax.random.fold_in(key, 11)
    key_noise = jax.random.fold_in(key, 1)
    key_mean = jax.random.fold_in(key, 2)
    key_gain = jax.random.fold_in(key, 3)
    shape = (NSNAP, 3, NX, NY, CZ)
    positions = jnp.arange(NX, dtype=jnp.float32) / NX
    component = (jnp.arange(3) == 0).astype(jnp.float32)[None, :, None, None, None]
    gains = jnp.exp(jax.random.uniform(key_gain, (NSNAP, 1, 1, 1, 1), jnp.float32, -0.7, 0.7))
    envelope = (3.0 ** positions)[None, None, :, None, None]
    noise_part = jnp.clip(jax.random.normal(key_noise, shape, jnp.float32), -5.0, 5.0)
    jet_mean = jax.random.uniform(key_mean, (NSNAP, 1, 1, 1, 1), jnp.float32, 0.5, 1.0)
    return (envelope * (gains * noise_part + component * jet_mean)).astype(jnp.float32)


def draw_sample_index(key, part):
    key = jax.random.fold_in(key, 23)
    offsets = jax.random.randint(key, (N_BRICK, N_ANA, SAMP_DEV), 0, 4)
    position = jnp.arange(SAMP_DEV, dtype=jnp.int32)
    offsets = jnp.where(position == 0, 0, jnp.where(position == SAMP_DEV - 1, 3, offsets))
    return (4 * position + offsets).astype(jnp.int32)


def draw_weighted_basis(key, part):
    key = jax.random.fold_in(key, 37)
    key_noise = jax.random.fold_in(key, 1)
    shape = (RANK, 3, ROWS)
    source = jnp.arange(ROWS) // SBLK % N_BRICK
    envelope = (10.0 ** (source.astype(jnp.float32) / N_BRICK))[None, None, :]
    singular = (3.0 * 10.0 ** (-jnp.arange(RANK, dtype=jnp.float32) / (RANK - 1)))[:, None, None]
    component = (jnp.arange(3) == 0).astype(jnp.float32)[None, :, None]
    noise_part = jnp.clip(jax.random.normal(key_noise, shape, jnp.float32), -5.0, 5.0)
    offset = 0.8
    return (singular * envelope * (noise_part + component * offset)).astype(jnp.float32)


def setup_inputs(seed: int = 0) -> dict:
    key_list = jax.random.split(jax.random.key(seed), 5)
    provisional = draw_provisional(jax.random.fold_in(key_list[4], 71), 0)
    sample_index = draw_sample_index(jax.random.fold_in(key_list[4], 71), 0)
    owner_table = jax.vmap(lambda own: jax.random.permutation(own, N_BRICK))(jax.random.split(key_list[2], N_BRICK)).reshape((N_BRICK, N_BRICK)).astype(jnp.int32)
    weighted_basis = draw_weighted_basis(jax.random.fold_in(key_list[4], 71), 0)
    return dict(provisional=provisional, sample_index=sample_index, owner_table=owner_table, weighted_basis=weighted_basis)


def depth_difference(grid_field):
    padded = jnp.pad(grid_field, [(0, 0)] * (grid_field.ndim - 1) + [(1, 1)])
    return 0.5 * (padded[..., 2:] - padded[..., :-2])

def depth_neighbours(grid_field):
    padded = jnp.pad(grid_field, [(0, 0)] * (grid_field.ndim - 1) + [(1, 1)])
    return padded[..., 2:] + padded[..., :-2]

def project_velocity(velocity):
    padded = jnp.pad(velocity, ((0, 0), (1, 1), (1, 1), (0, 0)))
    forcing = -(0.5 * (padded[0, 2:, 1:-1] - padded[0, :-2, 1:-1]) + 0.5 * (padded[1, 1:-1, 2:] - padded[1, 1:-1, :-2]) + depth_difference(velocity[2]))
    first_sweep = forcing / 6.0
    first_pad = jnp.pad(first_sweep, ((1, 1), (1, 1), (0, 0)))
    beside_all = first_pad[2:, 1:-1] + first_pad[:-2, 1:-1] + first_pad[1:-1, 2:] + first_pad[1:-1, :-2] + depth_neighbours(first_sweep)
    pressure = (forcing + beside_all) / 6.0
    pressure_pad = jnp.pad(pressure, ((1, 1), (1, 1), (0, 0)))
    gradient = jnp.stack([0.5 * (pressure_pad[2:, 1:-1] - pressure_pad[:-2, 1:-1]), 0.5 * (pressure_pad[1:-1, 2:] - pressure_pad[1:-1, :-2]), depth_difference(pressure)])
    return velocity - gradient

def reference(provisional, sample_index, owner_table, weighted_basis):
    send_order = jnp.argsort(owner_table, axis=1).astype(jnp.int32)
    chooser = jnp.broadcast_to(send_order[None, :, None, :, None], (3, N_BRICK, N_ANA, N_BRICK, SBLK)).astype(jnp.int32)
    picker = jnp.broadcast_to(sample_index[None], (3, N_BRICK, N_ANA, SAMP_DEV)).astype(jnp.int32)

    def one_snapshot(velocity):
        projected = project_velocity(velocity)
        blocks = projected.reshape(3, N_BRICK, CX, N_ANA, CY, CZ).transpose(0, 1, 3, 2, 4, 5)
        blocks = blocks.reshape(3, N_BRICK, N_ANA, CX * CY * CZ)
        picked = jnp.take_along_axis(blocks, picker, axis=3).reshape(3, N_BRICK, N_ANA, N_BRICK, SBLK)
        routed = jnp.take_along_axis(picked, chooser, axis=3)
        return routed.transpose(0, 3, 2, 1, 4).reshape(3, ROWS)
    samples = lax.map(one_snapshot, provisional)
    stacked = jnp.concatenate([weighted_basis, samples], axis=0).reshape(RANK + NSNAP, 3 * ROWS)
    gram_matrix = jnp.dot(stacked, stacked.T, precision=lax.Precision.HIGHEST) / (3.0 * ROWS)
    lower_factor = jnp.linalg.cholesky(gram_matrix)
    new_basis = jax.scipy.linalg.solve_triangular(lower_factor, stacked, lower=True)
    return (new_basis.reshape(RANK + NSNAP, 3, ROWS), lower_factor.T)
```

```python
import functools
import jax
import jax.numpy as jnp
from jax import lax
from jax.experimental import pallas as pl
from jax.experimental.pallas import tpu as pltpu
from jax.sharding import PartitionSpec as P

LANES = 128
PACK = 24
PARTS = 2
WIDTH = 8192


def split_rows(block, parts):
    pieces = []
    rest = block
    for step in range(parts):
        piece = rest.astype(jnp.bfloat16)
        pieces.append(piece)
        if step < parts - 1:
            rest = rest - piece.astype(jnp.float32)
    return jnp.concatenate(pieces, axis=0)


def sample_rows(arrived_ref):
    pieces = []
    for b in range(arrived_ref.shape[0]):
        for jj in range(8):
            pieces.append(arrived_ref[b, 0, 4 * jj : 4 * jj + 4, :])
    return jnp.concatenate(pieces, axis=1)


def stacked_block(basis_ref, arrived_ref):
    rows = sample_rows(arrived_ref)
    return jnp.concatenate([basis_ref[0], rows, jnp.zeros_like(rows)], axis=0)


def gram_kernel(parts, scale, basis_ref, arrived_ref, out_ref, total_ref):
    step = pl.program_id(0) * pl.num_programs(1) + pl.program_id(1)

    @pl.when(step == 0)
    def _():
        total_ref[...] = jnp.zeros_like(total_ref)

    pieces = split_rows(stacked_block(basis_ref, arrived_ref), parts)
    total_ref[...] += lax.dot_general(
        pieces, pieces, (((1,), (1,)), ((), ())), preferred_element_type=jnp.float32
    )

    @pl.when(step == pl.num_programs(0) * pl.num_programs(1) - 1)
    def _():
        total = total_ref[...]
        rows = sum(total[PACK * p : PACK * (p + 1)] for p in range(parts))
        gram = sum(rows[:, PACK * p : PACK * (p + 1)] for p in range(parts)) * scale
        gram = jnp.concatenate([gram, jnp.zeros((PACK, LANES - PACK), jnp.float32)], axis=1)
        packed = gram[0:8]
        packed = packed + pltpu.roll(gram[8:16], PACK, 1)
        packed = packed + pltpu.roll(gram[16:24], 2 * PACK, 1)
        out_ref[...] = jnp.broadcast_to(packed[None], out_ref.shape)


def factor(gram, count):
    row_at = lax.broadcasted_iota(jnp.int32, (PACK, LANES), 0)
    lane_at = lax.broadcasted_iota(jnp.int32, (PACK, LANES), 1)
    work = jnp.where(lane_at < PACK, gram, 0.0) + jnp.where(lane_at == row_at + 32, 1.0, 0.0)
    for j in range(count):
        pivot_row = work[j : j + 1]
        pivot = pivot_row[:, j : j + 1]
        ratio = work[:, j : j + 1] / pivot
        ratio = jnp.where(row_at[:, :1] > j, ratio, 0.0)
        work = work - ratio * pivot_row
    diagonal = jnp.sum(jnp.where(lane_at == row_at, work, 0.0), axis=1, keepdims=True)
    root = jnp.sqrt(jnp.where(row_at[:, :1] < count, diagonal, 1.0))
    work = work / root
    upper = jnp.where((lane_at >= row_at) & (lane_at < PACK), work, 0.0)
    inverse = pltpu.roll(work, LANES - 32, 1)[:, :PACK]
    return upper, inverse


def apply_kernel(parts, count, basis_ref, arrived_ref, packed_ref, out_ref, core_ref, left_ref):
    step = pl.program_id(0) * pl.num_programs(1) + pl.program_id(1)

    @pl.when(step == 0)
    def _():
        packed = jnp.sum(packed_ref[...], axis=0)
        gram = jnp.concatenate(
            [packed, pltpu.roll(packed, LANES - PACK, 1), pltpu.roll(packed, LANES - 2 * PACK, 1)],
            axis=0,
        )
        upper, inverse = factor(gram, count)
        core_ref[...] = upper
        left = split_rows(inverse, parts)
        left_ref[...] = jnp.concatenate([left] * parts, axis=1)

    pieces = split_rows(stacked_block(basis_ref, arrived_ref), parts)
    product = jnp.dot(left_ref[...], pieces, preferred_element_type=jnp.float32)
    result = sum(product[PACK * p : PACK * (p + 1)] for p in range(parts))
    out_ref[0] = result[: out_ref.shape[1]]


def tail(basis, arrived, parts, width, total_rows, devices):
    comps, rank_count, rows = basis.shape
    grid = (comps, rows // width)
    basis_spec = pl.BlockSpec((1, rank_count, width), lambda c, n: (c, 0, n))
    arrived_spec = pl.BlockSpec((width // 1024, 1, 32, LANES), lambda c, n: (n, c, 0, 0))
    params = pltpu.CompilerParams(vmem_limit_bytes=48 * 1024 * 1024)
    copies = pl.pallas_call(
        functools.partial(gram_kernel, parts, 1.0 / total_rows),
        grid=grid,
        in_specs=[basis_spec, arrived_spec],
        out_specs=pl.BlockSpec((devices, 8, LANES), lambda c, n: (0, 0, 0)),
        out_shape=jax.ShapeDtypeStruct((devices, 8, LANES), jnp.float32),
        scratch_shapes=[pltpu.VMEM((PACK * parts, PACK * parts), jnp.float32)],
        compiler_params=params,
        name="gram",
    )(basis, arrived)
    partial_sums = lax.all_to_all(copies, ("brick", "ana"), 0, 0, tiled=True)
    count = rank_count + 4
    return pl.pallas_call(
        functools.partial(apply_kernel, parts, count),
        grid=grid,
        in_specs=[
            basis_spec,
            arrived_spec,
            pl.BlockSpec((devices, 8, LANES), lambda c, n: (0, 0, 0)),
        ],
        out_specs=[
            pl.BlockSpec((1, count, width), lambda c, n: (c, 0, n)),
            pl.BlockSpec((PACK, LANES), lambda c, n: (0, 0)),
        ],
        out_shape=[
            jax.ShapeDtypeStruct((comps, count, rows), jnp.float32),
            jax.ShapeDtypeStruct((PACK, LANES), jnp.float32),
        ],
        scratch_shapes=[pltpu.VMEM((PACK * parts, PACK * parts), jnp.bfloat16)],
        compiler_params=params,
        name="apply",
    )(basis, arrived, partial_sums)


def padded_2(shard, sides, width):
    for axis, dim in sides:
        devices, length = (lax.axis_size(axis), shard.shape[dim])
        up = [(i, (i + 1) % devices) for i in range(devices - 1)]
        down = [(j, i) for i, j in up]
        last = lax.slice_in_dim(shard, length - width, length, axis=dim)
        first = lax.slice_in_dim(shard, 0, width, axis=dim)
        before = lax.ppermute(last, axis, up)
        after = lax.ppermute(first, axis, down)
        shard = jnp.concatenate([before, shard, after], axis=dim)
    return shard


def depth_difference(grid_field):
    padded = jnp.pad(grid_field, [(0, 0)] * (grid_field.ndim - 1) + [(1, 1)])
    return 0.5 * (padded[..., 2:] - padded[..., :-2])


def depth_neighbours(grid_field):
    padded = jnp.pad(grid_field, [(0, 0)] * (grid_field.ndim - 1) + [(1, 1)])
    return padded[..., 2:] + padded[..., :-2]


def divergence(padded):
    return (
        0.5 * (padded[:, 0, 2:, 1:-1] - padded[:, 0, :-2, 1:-1])
        + 0.5 * (padded[:, 1, 1:-1, 2:] - padded[:, 1, 1:-1, :-2])
        + depth_difference(padded[:, 2, 1:-1, 1:-1])
    )


def neighbour_sum(padded):
    return (
        padded[:, 2:, 1:-1]
        + padded[:, :-2, 1:-1]
        + padded[:, 1:-1, 2:]
        + padded[:, 1:-1, :-2]
        + depth_neighbours(padded[:, 1:-1, 1:-1])
    )


def pressure_gradient(padded):
    return jnp.stack(
        [
            0.5 * (padded[:, 2:, 1:-1] - padded[:, :-2, 1:-1]),
            0.5 * (padded[:, 1:-1, 2:] - padded[:, 1:-1, :-2]),
            depth_difference(padded[:, 1:-1, 1:-1]),
        ],
        axis=1,
    )


def select_samples(projected, chosen, samples_dev):
    snaps = projected.shape[0]
    depth = projected.shape[-1]
    offset = chosen - 4 * jnp.arange(samples_dev, dtype=jnp.int32)
    cell_mask = (offset[:, None] == jnp.arange(4, dtype=jnp.int32)[None, :]).reshape(-1, depth)
    grid_rows = projected.reshape(snaps, 3, -1, depth)
    kept = jnp.where(cell_mask[None, None], grid_rows, 0.0)
    pooling = (jnp.arange(depth)[:, None] // 4 == jnp.arange(depth // 4)[None, :]).astype(
        jnp.float32
    )
    picked = jnp.einsum("scrd,dk->scrk", kept, pooling, precision=lax.Precision.HIGHEST)
    return picked.reshape(snaps, 3, samples_dev)


def per_device(provisional, sample_index, owner_table, weighted_basis):
    snaps = provisional.shape[0]
    rank_count = weighted_basis.shape[0]
    samples_dev = sample_index.shape[2]
    bricks = lax.axis_size("brick")
    total_rows = 3.0 * samples_dev * bricks * lax.axis_size("ana")
    padded = padded_2(provisional, (("brick", 2), ("ana", 3)), 1)
    forcing = -divergence(padded)
    first_sweep = forcing / 6.0
    first_pad = padded_2(first_sweep, (("brick", 1), ("ana", 2)), 1)
    pressure = (forcing + neighbour_sum(first_pad)) / 6.0
    pressure_pad = padded_2(pressure, (("brick", 1), ("ana", 2)), 1)
    projected = provisional - pressure_gradient(pressure_pad)
    picked = select_samples(projected, sample_index[0, 0], samples_dev)
    owner_row = lax.dynamic_index_in_dim(owner_table, lax.axis_index("brick"), 0, keepdims=False)
    send_order = jnp.argsort(owner_row)
    blocks = picked.reshape(snaps, 3, bricks, samples_dev // bricks)
    outgoing = jnp.take(blocks, send_order, axis=2)
    outgoing = outgoing.reshape(snaps, 3, bricks, 8, LANES).transpose(2, 1, 3, 0, 4)
    outgoing = outgoing.reshape(bricks, 3, 32, LANES)
    arrived = lax.all_to_all(outgoing, "brick", split_axis=0, concat_axis=0, tiled=True)
    basis = jnp.transpose(weighted_basis, (1, 0, 2))
    devices = bricks * lax.axis_size("ana")
    new_basis, core = tail(basis, arrived, PARTS, WIDTH, total_rows, devices)
    count = rank_count + snaps
    return (jnp.transpose(new_basis, (1, 0, 2)), core[:count, :count])


def solution(mesh):
    placed = (
        P(None, None, "brick", "ana", None),
        P("brick", "ana", None),
        P(),
        P(None, None, ("brick", "ana")),
    )
    return jax.shard_map(
        per_device,
        mesh=mesh,
        in_specs=placed,
        out_specs=(P(None, None, ("brick", "ana")), P()),
        check_vma=False,
    )
```

```python
import functools
import jax
import jax.numpy as jnp
from jax import lax
from jax.experimental import pallas as pl
from jax.experimental.pallas import tpu as pltpu
from jax.sharding import PartitionSpec as P

LANES = 128
PACK = 24
PARTS = 2
POOL_PARTS = 2
WIDTH = 8192


def split_rows(block, parts):
    pieces = []
    rest = block
    for step in range(parts):
        piece = rest.astype(jnp.bfloat16)
        pieces.append(piece)
        if step < parts - 1:
            rest = rest - piece.astype(jnp.float32)
    return jnp.concatenate(pieces, axis=0)


def sample_rows(arrived_ref):
    pieces = []
    for b in range(arrived_ref.shape[0]):
        for jj in range(8):
            pieces.append(arrived_ref[b, 0, 4 * jj : 4 * jj + 4, :])
    return jnp.concatenate(pieces, axis=1)


def stacked_block(basis_ref, arrived_ref):
    rows = sample_rows(arrived_ref)
    return jnp.concatenate([basis_ref[0], rows, jnp.zeros_like(rows)], axis=0)


def gram_kernel(parts, scale, basis_ref, arrived_ref, out_ref, total_ref):
    step = pl.program_id(0) * pl.num_programs(1) + pl.program_id(1)

    @pl.when(step == 0)
    def _():
        total_ref[...] = jnp.zeros_like(total_ref)

    pieces = split_rows(stacked_block(basis_ref, arrived_ref), parts)
    total_ref[...] += lax.dot_general(
        pieces, pieces, (((1,), (1,)), ((), ())), preferred_element_type=jnp.float32
    )

    @pl.when(step == pl.num_programs(0) * pl.num_programs(1) - 1)
    def _():
        total = total_ref[...]
        rows = sum(total[PACK * p : PACK * (p + 1)] for p in range(parts))
        gram = sum(rows[:, PACK * p : PACK * (p + 1)] for p in range(parts)) * scale
        gram = jnp.concatenate([gram, jnp.zeros((PACK, LANES - PACK), jnp.float32)], axis=1)
        packed = gram[0:8]
        packed = packed + pltpu.roll(gram[8:16], PACK, 1)
        packed = packed + pltpu.roll(gram[16:24], 2 * PACK, 1)
        out_ref[...] = jnp.broadcast_to(packed[None], out_ref.shape)


def factor(gram, count):
    row_at = lax.broadcasted_iota(jnp.int32, (PACK, LANES), 0)
    lane_at = lax.broadcasted_iota(jnp.int32, (PACK, LANES), 1)
    work = jnp.where(lane_at < PACK, gram, 0.0) + jnp.where(lane_at == row_at + 32, 1.0, 0.0)
    for j in range(count):
        pivot_row = work[j : j + 1]
        pivot = pivot_row[:, j : j + 1]
        ratio = work[:, j : j + 1] / pivot
        ratio = jnp.where(row_at[:, :1] > j, ratio, 0.0)
        work = work - ratio * pivot_row
    diagonal = jnp.sum(jnp.where(lane_at == row_at, work, 0.0), axis=1, keepdims=True)
    root = jnp.sqrt(jnp.where(row_at[:, :1] < count, diagonal, 1.0))
    work = work / root
    upper = jnp.where((lane_at >= row_at) & (lane_at < PACK), work, 0.0)
    inverse = pltpu.roll(work, LANES - 32, 1)[:, :PACK]
    return upper, inverse


def apply_kernel(parts, count, basis_ref, arrived_ref, packed_ref, out_ref, core_ref, left_ref):
    step = pl.program_id(0) * pl.num_programs(1) + pl.program_id(1)

    @pl.when(step == 0)
    def _():
        packed = jnp.sum(packed_ref[...], axis=0)
        gram = jnp.concatenate(
            [packed, pltpu.roll(packed, LANES - PACK, 1), pltpu.roll(packed, LANES - 2 * PACK, 1)],
            axis=0,
        )
        upper, inverse = factor(gram, count)
        core_ref[...] = upper
        left = split_rows(inverse, parts)
        left_ref[...] = jnp.concatenate([left] * parts, axis=1)

    pieces = split_rows(stacked_block(basis_ref, arrived_ref), parts)
    product = jnp.dot(left_ref[...], pieces, preferred_element_type=jnp.float32)
    result = sum(product[PACK * p : PACK * (p + 1)] for p in range(parts))
    out_ref[0] = result[: out_ref.shape[1]]


def tail(basis, arrived, parts, width, total_rows, devices):
    comps, rank_count, rows = basis.shape
    grid = (comps, rows // width)
    basis_spec = pl.BlockSpec((1, rank_count, width), lambda c, n: (c, 0, n))
    arrived_spec = pl.BlockSpec((width // 1024, 1, 32, LANES), lambda c, n: (n, c, 0, 0))
    params = pltpu.CompilerParams(vmem_limit_bytes=48 * 1024 * 1024)
    copies = pl.pallas_call(
        functools.partial(gram_kernel, parts, 1.0 / total_rows),
        grid=grid,
        in_specs=[basis_spec, arrived_spec],
        out_specs=pl.BlockSpec((devices, 8, LANES), lambda c, n: (0, 0, 0)),
        out_shape=jax.ShapeDtypeStruct((devices, 8, LANES), jnp.float32),
        scratch_shapes=[pltpu.VMEM((PACK * parts, PACK * parts), jnp.float32)],
        compiler_params=params,
        name="gram",
    )(basis, arrived)
    partial_sums = lax.all_to_all(copies, ("brick", "ana"), 0, 0, tiled=True)
    count = rank_count + 4
    return pl.pallas_call(
        functools.partial(apply_kernel, parts, count),
        grid=grid,
        in_specs=[
            basis_spec,
            arrived_spec,
            pl.BlockSpec((devices, 8, LANES), lambda c, n: (0, 0, 0)),
        ],
        out_specs=[
            pl.BlockSpec((1, count, width), lambda c, n: (c, 0, n)),
            pl.BlockSpec((PACK, LANES), lambda c, n: (0, 0)),
        ],
        out_shape=[
            jax.ShapeDtypeStruct((comps, count, rows), jnp.float32),
            jax.ShapeDtypeStruct((PACK, LANES), jnp.float32),
        ],
        scratch_shapes=[pltpu.VMEM((PACK * parts, PACK * parts), jnp.bfloat16)],
        compiler_params=params,
        name="apply",
    )(basis, arrived, partial_sums)


ANA_ROWS = 56
BRICK_ROWS = 104


def depth_pair(field):
    lanes = field.shape[-1]
    lane_at = lax.broadcasted_iota(jnp.int32, field.shape, field.ndim - 1)
    after = jnp.where(lane_at == lanes - 1, 0.0, pltpu.roll(field, lanes - 1, field.ndim - 1))
    before = jnp.where(lane_at == 0, 0.0, pltpu.roll(field, 1, field.ndim - 1))
    return after, before


def row_pair(field, after_row, before_row):
    rows = field.shape[0]
    row_at = lax.broadcasted_iota(jnp.int32, field.shape, 0)
    after = jnp.where(row_at == rows - 1, after_row, pltpu.roll(field, rows - 1, 0))
    before = jnp.where(row_at == 0, before_row, pltpu.roll(field, 1, 0))
    return after, before


def difference(pair):
    return pair[0] - pair[1]


def ana_edge_kernel(low_ref, high_ref, to_low_ref, to_high_ref):
    snaps = to_low_ref.shape[0]
    comps, layers, rows, lanes = low_ref.shape
    flat = (comps * layers * rows, lanes)
    low, high = low_ref.reshape(*flat), high_ref.reshape(*flat)

    def column(ref, s, c, j):
        start = (s * 3 + c) * layers * rows + j
        return jnp.concatenate(
            [ref[pl.ds(start + 8 * half, layers, stride=rows), :] for half in range(2)], axis=1
        )

    zero_row = jnp.zeros((1, 2 * lanes), jnp.float32)
    for s in range(snaps):
        for ref, out_ref, edge, second, third, sign in (
            (low, to_low_ref, 0, 1, 2, 1.0),
            (high, to_high_ref, 7, 6, 5, -1.0),
        ):
            speed = [column(ref, s, 0, j) for j in (edge, second)]
            cross = [column(ref, s, 1, j) for j in (edge, second, third)]
            deep = [column(ref, s, 2, j) for j in (edge, second)]
            beside = (sign * cross[1], sign * (cross[2] - cross[0]))
            out_ref[s, 0:16, :] = cross[0]
            for n in range(2):
                along = difference(row_pair(speed[n], zero_row, zero_row))
                out_ref[s, 16 + 16 * n : 32 + 16 * n, :] = -0.5 * (
                    along + beside[n] + difference(depth_pair(deep[n]))
                )
            out_ref[s, 48:56, :] = jnp.concatenate(
                [speed[0][0:1], speed[1][0:1], speed[0][15:16], speed[1][15:16]] + [zero_row] * 4,
                axis=0,
            )


def brick_edge_kernel(bounds_ref, first_ref, last_ref, from_low_ref, from_high_ref, to_low_ref, to_high_ref):
    keep_low, keep_high = bounds_ref[2] > 0, bounds_ref[3] > 0
    for s in range(to_low_ref.shape[0]):
        for ref, out_ref, edge, second, third, sign, layer, pillar in (
            (first_ref, to_low_ref, 0, 1, 2, 1.0, 0, 48),
            (last_ref, to_high_ref, 3, 2, 1, -1.0, 15, 50),
        ):
            other = layer + 1 if layer == 0 else layer - 1

            def halo(side_ref, keep, row):
                return jnp.where(keep, side_ref[s, row : row + 1, :], 0.0)

            def force(at, i, along):
                cross = ref[3 * s + 1, at]
                pair = row_pair(cross, halo(from_high_ref, keep_high, i), halo(from_low_ref, keep_low, i))
                return -0.5 * (along + difference(pair) + difference(depth_pair(ref[3 * s + 2, at])))

            speed = ref[3 * s, edge]
            cross = ref[3 * s + 1, edge]
            out_ref[s, 0:32, :] = force(second, other, sign * (ref[3 * s, third] - speed))
            out_ref[s, 32:64, :] = force(edge, layer, sign * ref[3 * s, second])
            out_ref[s, 64:96, :] = speed
            below = jnp.where(keep_low, from_low_ref[s, 16 + layer : 17 + layer, :] - 0.5 * cross[0:1], 0.0)
            above = jnp.where(keep_high, from_high_ref[s, 16 + layer : 17 + layer, :] + 0.5 * cross[31:32], 0.0)
            out_ref[s, 96:104, :] = jnp.concatenate(
                [
                    halo(from_low_ref, keep_low, pillar + 1),
                    halo(from_low_ref, keep_low, pillar),
                    halo(from_high_ref, keep_high, pillar),
                    halo(from_high_ref, keep_high, pillar + 1),
                    below,
                    above,
                    jnp.zeros_like(below),
                    jnp.zeros_like(below),
                ],
                axis=0,
            )


def project_kernel(
    parts, bounds_ref, owner_ref, velocity_ref, weight_ref, pool_ref,
    low_ref, high_ref, before_ref, after_ref, out_ref,
    force_ref, press_ref, side_force_ref, side_press_ref, split_ref, pooled_ref,
):
    s = pl.program_id(0)
    layers = velocity_ref.shape[1]
    keep_before, keep_after = bounds_ref[0] > 0, bounds_ref[1] > 0
    keep_low, keep_high = bounds_ref[2] > 0, bounds_ref[3] > 0

    def halo(ref, keep, start, size=1):
        return jnp.where(keep, ref[0, start : start + size, :], 0.0)

    for i in range(layers):
        ahead = velocity_ref[0, i + 1] if i < layers - 1 else halo(after_ref, keep_after, 64, 32)
        behind = velocity_ref[0, i - 1] if i > 0 else halo(before_ref, keep_before, 64, 32)
        cross = row_pair(velocity_ref[1, i], halo(high_ref, keep_high, i), halo(low_ref, keep_low, i))
        force_ref[i + 2] = -0.5 * (
            (ahead - behind) + difference(cross) + difference(depth_pair(velocity_ref[2, i]))
        )
    force_ref[0] = halo(before_ref, keep_before, 0, 32)
    force_ref[1] = jnp.where(keep_before, before_ref[0, 32:64, :] - 0.5 * velocity_ref[0, 0], 0.0)
    force_ref[layers + 2] = jnp.where(
        keep_after, after_ref[0, 32:64, :] + 0.5 * velocity_ref[0, layers - 1], 0.0
    )
    force_ref[layers + 3] = halo(after_ref, keep_after, 0, 32)

    for side, ref, keep, pillar, far, near, corner, row, sign in (
        (0, low_ref, keep_low, 48, 96, 97, 100, 0, -0.5),
        (1, high_ref, keep_high, 48, 99, 98, 101, 31, 0.5),
    ):
        own_cross = jnp.concatenate([velocity_ref[1, i, row : row + 1, :] for i in range(layers)], axis=0)
        own_force = jnp.concatenate([force_ref[i + 2, row : row + 1, :] for i in range(layers)], axis=0)
        row_at = lax.broadcasted_iota(jnp.int32, own_force.shape, 0)

        def ends(before_row, after_row):
            first = 0.5 * halo(before_ref, keep_before, before_row)
            last = -0.5 * halo(after_ref, keep_after, after_row)
            return jnp.where(row_at == 0, first, 0.0) + jnp.where(row_at == layers - 1, last, 0.0)

        edge = jnp.where(keep, ref[0, 16:32, :] + sign * own_cross + ends(near, near), 0.0)
        beyond = jnp.where(keep, ref[0, 32:48, :] + ends(far, far), 0.0)
        corner_before = jnp.where(
            keep_before, halo(before_ref, keep, corner) - 0.5 * halo(ref, keep, pillar), 0.0
        )
        corner_after = jnp.where(
            keep_after, halo(after_ref, keep, corner) + 0.5 * halo(ref, keep, pillar + 2), 0.0
        )
        around = sum(row_pair(edge, corner_after, corner_before)) + beyond + own_force
        around = around + sum(depth_pair(edge))
        press = (edge + around * (1.0 / 6.0)) * (1.0 / 6.0)
        side_press_ref[side] = jnp.where(keep, press, 0.0)
        side_force_ref[side, 8:24, :] = edge
        side_force_ref[side, 7:8, :] = corner_before
        side_force_ref[side, 24:25, :] = corner_after

    for i in range(-1, layers + 1):
        field = force_ref[i + 2]
        beside = row_pair(field, side_force_ref[1, 8 + i : 9 + i, :], side_force_ref[0, 8 + i : 9 + i, :])
        around = (force_ref[i + 3] + force_ref[i + 1]) + sum(beside) + sum(depth_pair(field))
        press = (field + around * (1.0 / 6.0)) * (1.0 / 6.0)
        if i == -1:
            press = jnp.where(keep_before, press, 0.0)
        if i == layers:
            press = jnp.where(keep_after, press, 0.0)
        press_ref[i + 1] = press

    for i in range(layers):
        press = press_ref[i + 1]
        beside = row_pair(press, side_press_ref[1, i : i + 1, :], side_press_ref[0, i : i + 1, :])
        gradient = (press_ref[i + 2] - press_ref[i], difference(beside), difference(depth_pair(press)))
        weight = weight_ref[32 * i : 32 * i + 32, :]
        for c in range(3):
            kept = (velocity_ref[c, i] - 0.5 * gradient[c]) * weight
            for p in range(parts):
                piece = kept.astype(jnp.bfloat16)
                split_ref[32 * i : 32 * i + 32, 256 * p : 256 * p + 256] = piece
                if p < parts - 1:
                    kept = kept - piece.astype(jnp.float32)
            split = split_ref[32 * i : 32 * i + 32, :]
            pooled = jnp.dot(split, pool_ref[...], preferred_element_type=jnp.float32)
            pooled_ref[0, c, 32 * i : 32 * i + 32, :] = pooled[:, :LANES]
            pooled_ref[1, c, 32 * i : 32 * i + 32, :] = pooled[:, LANES:]

    flat = pooled_ref.reshape(2 * 3 * 32 * layers, LANES)
    out_flat = out_ref.reshape(out_ref.shape[0] * 3 * 32, LANES)
    for k in range(2 * layers):
        owner = owner_ref[k]
        for c in range(3):
            start = c * 32 * layers + 16 * k
            tile = flat[pl.ds(start, 8, stride=2), :] + flat[pl.ds(start + 3 * 32 * layers + 1, 8, stride=2), :]
            out_flat[pl.ds((owner * 3 + c) * 32 + s, 8, stride=4), :] = tile


def weight_kernel(index_ref, out_ref, wide_ref):
    rows = index_ref.shape[0]
    at = lax.broadcasted_iota(jnp.int32, (rows, LANES), 0) * LANES + lax.broadcasted_iota(jnp.int32, (rows, LANES), 1)
    offset = (index_ref[...] - 4 * at).astype(jnp.float32).astype(jnp.bfloat16)
    source = lax.broadcasted_iota(jnp.int32, (LANES, 512), 0)
    target = lax.broadcasted_iota(jnp.int32, (LANES, 512), 1)
    expand = jnp.where(target // 4 == source, 1.0, 0.0).astype(jnp.bfloat16)
    wide = jnp.dot(offset, expand, preferred_element_type=jnp.float32)
    lane_at = lax.broadcasted_iota(jnp.int32, wide.shape, 1)
    hit = jnp.where(wide == (lane_at % 4).astype(jnp.float32), 1.0, 0.0)
    for half in range(2):
        for kt in range(2):
            wide_ref[kt, pl.ds(half, rows, stride=2), :] = hit[:, 256 * half + 128 * kt : 256 * half + 128 * kt + 128]
    for kt in range(2):
        out_ref[:, 128 * kt : 128 * kt + 128] = wide_ref[kt]


def pooling(parts):
    source = lax.broadcasted_iota(jnp.int32, (256 * parts, 256), 0) % 256
    target = lax.broadcasted_iota(jnp.int32, (256 * parts, 256), 1)
    low = (target < 64) & (source // 4 == target)
    high = (target >= 192) & (source // 4 == target - 192)
    return jnp.where(low | high, 1.0, 0.0).astype(jnp.bfloat16)


def ring(devices):
    up = [(i, (i + 1) % devices) for i in range(devices)]
    return up, [(j, i) for i, j in up]


def exchange(to_before, to_after, axis):
    up, down = ring(lax.axis_size(axis))
    return lax.ppermute(to_after, axis, up), lax.ppermute(to_before, axis, down)


def whole(shape):
    return pl.BlockSpec(shape, lambda *_: (0,) * len(shape))


def front(provisional, sample_index, owner_table):
    snaps, comps, layers, columns, depth = provisional.shape
    bricks, anas = lax.axis_size("brick"), lax.axis_size("ana")
    b, a = lax.axis_index("brick"), lax.axis_index("ana")
    bounds = jnp.stack([b, bricks - 1 - b, a, anas - 1 - a]).astype(jnp.int32)
    owner = lax.dynamic_index_in_dim(owner_table, b, 0, keepdims=False)
    params = pltpu.CompilerParams(vmem_limit_bytes=48 * 1024 * 1024)
    smem = pl.BlockSpec(memory_space=pltpu.SMEM)
    samples = layers * columns * depth // 4
    fields = provisional.reshape(snaps * comps, layers, columns, depth)

    tiles = fields.reshape(snaps * comps, layers, columns // 8, 8, 2, LANES)
    tiles = tiles.transpose(0, 1, 2, 4, 3, 5).reshape(snaps * comps, layers, columns // 8, 16, LANES)
    tile_spec = lambda at: pl.BlockSpec((snaps * comps, layers, None, 16, LANES), lambda n: (0, 0, at, 0, 0))
    ana_shape = jax.ShapeDtypeStruct((snaps, ANA_ROWS, depth), jnp.float32)
    to_low, to_high = pl.pallas_call(
        ana_edge_kernel,
        grid=(1,),
        in_specs=[tile_spec(0), tile_spec(columns // 8 - 1)],
        out_specs=[whole(ana_shape.shape)] * 2,
        out_shape=[ana_shape] * 2,
        compiler_params=params,
        name="ana_edges",
    )(tiles, tiles)
    from_low, from_high = exchange(to_low, to_high, "ana")

    weight = pl.pallas_call(
        weight_kernel,
        in_specs=[whole((samples // LANES, LANES))],
        out_specs=whole((layers * columns, depth)),
        out_shape=jax.ShapeDtypeStruct((layers * columns, depth), jnp.float32),
        grid=(1,),
        scratch_shapes=[pltpu.VMEM((2, layers * columns, LANES), jnp.float32)],
        compiler_params=params,
        name="weights",
    )(sample_index.reshape(samples // LANES, LANES))

    brick_shape = jax.ShapeDtypeStruct((snaps, BRICK_ROWS, depth), jnp.float32)
    layer_spec = lambda at: pl.BlockSpec((snaps * comps, 4, columns, depth), lambda n: (0, at, 0, 0))
    to_before, to_after = pl.pallas_call(
        brick_edge_kernel,
        grid=(1,),
        in_specs=[smem, layer_spec(0), layer_spec(layers // 4 - 1), whole(ana_shape.shape), whole(ana_shape.shape)],
        out_specs=[whole(brick_shape.shape)] * 2,
        out_shape=[brick_shape] * 2,
        compiler_params=params,
        name="brick_edges",
    )(bounds, fields, fields, from_low, from_high)
    from_before, from_after = exchange(to_before, to_after, "brick")

    one = lambda shape: pl.BlockSpec((1,) + shape[1:], lambda n: (n, 0, 0))
    return pl.pallas_call(
        functools.partial(project_kernel, POOL_PARTS),
        grid=(snaps,),
        in_specs=[
            smem,
            smem,
            pl.BlockSpec((comps, layers, columns, depth), lambda n: (n, 0, 0, 0)),
            whole((layers * columns, depth)),
            whole((256 * POOL_PARTS, 256)),
            one(ana_shape.shape),
            one(ana_shape.shape),
            one(brick_shape.shape),
            one(brick_shape.shape),
        ],
        out_specs=whole((bricks, comps, 32, LANES)),
        out_shape=jax.ShapeDtypeStruct((bricks, comps, 32, LANES), jnp.float32),
        scratch_shapes=[
            pltpu.VMEM((layers + 4, columns, depth), jnp.float32),
            pltpu.VMEM((layers + 2, columns, depth), jnp.float32),
            pltpu.VMEM((2, 32, depth), jnp.float32),
            pltpu.VMEM((2, layers, depth), jnp.float32),
            pltpu.VMEM((layers * columns, 256 * POOL_PARTS), jnp.bfloat16),
            pltpu.VMEM((2, comps, layers * columns, LANES), jnp.float32),
        ],
        compiler_params=params,
        name="project",
    )(bounds, owner, fields, weight, pooling(POOL_PARTS), from_low, from_high, from_before, from_after)


def per_device(provisional, sample_index, owner_table, weighted_basis):
    snaps = provisional.shape[0]
    rank_count = weighted_basis.shape[0]
    devices = lax.axis_size("brick") * lax.axis_size("ana")
    total_rows = 3.0 * sample_index.shape[2] * devices
    outgoing = front(provisional, sample_index, owner_table)
    arrived = lax.all_to_all(outgoing, "brick", split_axis=0, concat_axis=0, tiled=True)
    basis = jnp.transpose(weighted_basis, (1, 0, 2))
    new_basis, core = tail(basis, arrived, PARTS, WIDTH, total_rows, devices)
    count = rank_count + snaps
    return (jnp.transpose(new_basis, (1, 0, 2)), core[:count, :count])


def solution(mesh):
    placed = (
        P(None, None, "brick", "ana", None),
        P("brick", "ana", None),
        P(),
        P(None, None, ("brick", "ana")),
    )
    return jax.shard_map(
        per_device,
        mesh=mesh,
        in_specs=placed,
        out_specs=(P(None, None, ("brick", "ana")), P()),
        check_vma=False,
    )
```

```python
import functools
import jax
import jax.numpy as jnp
from jax import lax
from jax.experimental import pallas as pl
from jax.experimental.pallas import tpu as pltpu
from jax.sharding import PartitionSpec as P

LANES = 128
PACK = 24
POOL_PARTS = 2
WIDTH = 8192
SLOTS = 4
VMEM_LIMIT = 20 * 1024 * 1024


def split_pieces(block):
    high = block.astype(jnp.bfloat16)
    return high, (block - high.astype(jnp.float32)).astype(jnp.bfloat16)


def stacked_pieces(basis_ref, arrived_ref, c, start, width, order):
    rows = jnp.concatenate(
        [
            arrived_ref[b, c, 4 * jj : 4 * jj + 4, :]
            for b in range(start // 1024, (start + width) // 1024)
            for jj in range(8)
        ],
        axis=1,
    )
    small = split_pieces(rows)
    small = [small[p].astype(jnp.float32) for p in order] + [jnp.zeros_like(rows)] * (4 - len(order))
    small = jnp.concatenate(small, axis=0).astype(jnp.bfloat16)
    large = split_pieces(basis_ref[c, :, start : start + width])
    return jnp.concatenate([large[p] for p in order] + [small], axis=0)


def gram_kernel(width, scale, basis_ref, arrived_ref, out_ref):
    comps, rank_count, columns = basis_ref.shape
    parts = 2
    total = 0.0
    for c in range(comps):
        for start in range(0, columns, width):
            pieces = stacked_pieces(basis_ref, arrived_ref, c, start, width, (0, 1))
            total = total + lax.dot_general(
                pieces, pieces, (((1,), (1,)), ((), ())), preferred_element_type=jnp.float32
            )
    base = rank_count * parts
    rows = sum(total[rank_count * p : rank_count * (p + 1)] for p in range(parts))
    small = sum(total[base + 4 * p : base + 4 * (p + 1)] for p in range(parts))
    rows = jnp.concatenate([rows, small, jnp.zeros_like(small)], axis=0)
    left = sum(rows[:, rank_count * p : rank_count * (p + 1)] for p in range(parts))
    right = sum(rows[:, base + 4 * p : base + 4 * (p + 1)] for p in range(parts))
    rest = jnp.zeros((PACK, LANES - rank_count - 4), jnp.float32)
    gram = jnp.concatenate([left, right, rest], axis=1) * scale
    packed = gram[0:4]
    for n in range(1, 5):
        packed = packed + pltpu.roll(gram[4 * n : 4 * n + 4], n * PACK, 1)
    out_ref[...] = jnp.broadcast_to(packed[None], out_ref.shape)


def factor(tiles, count):
    row_at = [lax.broadcasted_iota(jnp.int32, (8, LANES), 0) + 8 * t for t in range(3)]
    lane_at = lax.broadcasted_iota(jnp.int32, (8, LANES), 1)
    work = [jnp.where(lane_at < PACK, tiles[t], 0.0) + jnp.where(lane_at == row_at[t] + 32, 1.0, 0.0) for t in range(3)]
    roots = []
    block = 4
    for j in range(0, count, block):
        t0, r0 = j // 8, j % 8
        rows = [jnp.broadcast_to(work[t0][r0 + q : r0 + q + 1], (8, LANES)) for q in range(block)]
        cols = [[jnp.broadcast_to(work[t][:, j + q : j + q + 1], (8, LANES)) for t in range(3)] for q in range(block)]
        pivots = [
            [jnp.broadcast_to(work[t0][r0 + q : r0 + q + 1, j + r : j + r + 1], (8, LANES)) for r in range(block)]
            for q in range(block)
        ]
        for q in range(block):
            inverse = 1.0 / pivots[q][q]
            roots.append(pivots[q][q])
            for r in range(q + 1, block):
                ratio = pivots[r][q] * inverse
                across = pivots[q][r] * inverse
                rows[r] = rows[r] - ratio * rows[q]
                for t in range(t0, 3):
                    cols[r][t] = cols[r][t] - cols[q][t] * across
                for u in range(q + 1, block):
                    pivots[r][u] = pivots[r][u] - ratio * pivots[q][u]
            for t in range(t0, 3):
                ratio = jnp.where(row_at[t] > j + q, cols[q][t] * inverse, 0.0)
                work[t] = work[t] - ratio * rows[q]
    for t in range(3):
        diagonal = jnp.ones((8, LANES), jnp.float32)
        for j in range(8 * t, min(count, 8 * t + 8)):
            diagonal = jnp.where(row_at[t] == j, roots[j], diagonal)
        work[t] = work[t] / jnp.sqrt(diagonal)
    upper = [jnp.where((lane_at >= row_at[t]) & (lane_at < PACK), work[t], 0.0) for t in range(3)]
    inverse = jnp.concatenate([pltpu.roll(work[t], LANES - 32, 1)[:, :PACK] for t in range(3)], axis=0)
    return upper, inverse


def apply_kernel(width, slots, basis_ref, arrived_ref, packed_ref, out_ref, core_ref, left_ref, slot_ref, sem):
    comps, rank_count, columns = basis_ref.shape
    count = out_ref.shape[1]
    packed = jnp.sum(packed_ref[...], axis=0)
    parts = [packed] + [pltpu.roll(packed, LANES - n * PACK, 1) for n in range(1, 5)] + [jnp.zeros_like(packed)]
    tiles = [jnp.concatenate(parts[2 * t : 2 * t + 2], axis=0) for t in range(3)]
    upper, inverse = factor(tiles, count)
    for t in range(3):
        core_ref[8 * t : 8 * t + 8, :] = upper[t]
    high, low = [piece.astype(jnp.float32) for piece in split_pieces(inverse)]
    order = (high, high, low)
    left = [piece[:, :rank_count] for piece in order] + [piece[:, rank_count:count] for piece in order]
    left.append(jnp.zeros((PACK, 16 - 4 * len(order)), jnp.float32))
    left_ref[...] = jnp.concatenate(left, axis=1).astype(jnp.bfloat16)

    blocks = [(c, start) for c in range(comps) for start in range(0, columns, width)]
    copies = []
    for n, (c, start) in enumerate(blocks):
        if n >= slots:
            copies[n - slots].wait()
        pieces = stacked_pieces(basis_ref, arrived_ref, c, start, width, (0, 1, 0))
        product = jnp.dot(left_ref[...], pieces, preferred_element_type=jnp.float32)
        slot = n % slots
        slot_ref[slot] = product[:count]
        copy = pltpu.make_async_copy(slot_ref.at[slot], out_ref.at[c, :, start : start + width], sem.at[slot])
        copy.start()
        copies.append(copy)
    for copy in copies[-slots:]:
        copy.wait()


def tail(basis, arrived, width, total_rows, devices):
    comps, rank_count, rows = basis.shape
    vmem = pl.BlockSpec(memory_space=pltpu.VMEM)
    copies = grid_kernel(
        functools.partial(gram_kernel, width, 1.0 / total_rows),
        "gram",
        (10**9, 10**7),
        in_specs=[vmem, vmem],
        out_specs=vmem,
        out_shape=jax.ShapeDtypeStruct((devices, 4, LANES), jnp.float32),
    )(basis, arrived)
    partial_sums = lax.all_to_all(copies, ("brick", "ana"), 0, 0, tiled=True)
    count = rank_count + 4
    return grid_kernel(
        functools.partial(apply_kernel, width, SLOTS),
        "apply",
        (10**9, 2 * 10**7),
        in_specs=[vmem] * 3,
        out_specs=[pl.BlockSpec(memory_space=pltpu.HBM), vmem],
        out_shape=[
            jax.ShapeDtypeStruct((comps, count, rows), jnp.float32),
            jax.ShapeDtypeStruct((PACK, LANES), jnp.float32),
        ],
        scratch_shapes=[
            pltpu.VMEM((PACK, rank_count * 3 + 16), jnp.bfloat16),
            pltpu.VMEM((SLOTS, count, width), jnp.float32),
            pltpu.SemaphoreType.DMA((SLOTS,)),
        ],
    )(basis, arrived, partial_sums)


ANA_ROWS = 56
BULK_ROWS = 96
FIX_ROWS = 16
MARGIN = 3


def depth_pair(field):
    lanes = field.shape[-1]
    lane_at = lax.broadcasted_iota(jnp.int32, field.shape, field.ndim - 1)
    after = jnp.where(lane_at == lanes - 1, 0.0, pltpu.roll(field, lanes - 1, field.ndim - 1))
    before = jnp.where(lane_at == 0, 0.0, pltpu.roll(field, 1, field.ndim - 1))
    return after, before


def row_pair(field, after_row, before_row):
    rows = field.shape[0]
    row_at = lax.broadcasted_iota(jnp.int32, field.shape, 0)
    after = jnp.where(row_at == rows - 1, after_row, pltpu.roll(field, rows - 1, 0))
    before = jnp.where(row_at == 0, before_row, pltpu.roll(field, 1, 0))
    return after, before


def inside(axis):
    at = lax.axis_index(axis)
    return at > 0, at < lax.axis_size(axis) - 1


def difference(pair):
    return pair[0] - pair[1]


def relaxed(field, around):
    return (field + around * (1.0 / 6.0)) * (1.0 / 6.0)


def ana_edge_kernel(tiles_ref, to_low_ref, to_high_ref, low_ref, high_ref, sem):
    snaps = to_low_ref.shape[0]
    fields, layers, rows, lanes = low_ref.shape
    last = tiles_ref.shape[2] - 1
    copies = [
        pltpu.make_async_copy(tiles_ref.at[:, :, at], ref, sem.at[n])
        for n, (at, ref) in enumerate(((0, low_ref), (last, high_ref)))
    ]
    for copy in copies:
        copy.start()
    flat = (fields * layers * rows, lanes)

    def column(ref, s, c, j):
        start = (s * 3 + c) * layers * rows + j
        return jnp.concatenate(
            [ref[pl.ds(start + 8 * half, layers, stride=rows), :] for half in range(2)], axis=1
        )

    zero_row = jnp.zeros((1, 2 * lanes), jnp.float32)
    for copy, side_ref, out_ref, edge, second, third, sign in (
        (copies[0], low_ref, to_low_ref, 0, 1, 2, 1.0),
        (copies[1], high_ref, to_high_ref, 7, 6, 5, -1.0),
    ):
        copy.wait()
        ref = side_ref.reshape(*flat)
        for s in range(snaps):
            speed = [column(ref, s, 0, j) for j in (edge, second)]
            cross = [column(ref, s, 1, j) for j in (edge, second, third)]
            deep = [column(ref, s, 2, j) for j in (edge, second)]
            beside = (sign * cross[1], sign * (cross[2] - cross[0]))
            out_ref[s, 0:16, :] = cross[0]
            for n in range(2):
                along = difference(row_pair(speed[n], zero_row, zero_row))
                out_ref[s, 16 + 16 * n : 32 + 16 * n, :] = -0.5 * (
                    along + beside[n] + difference(depth_pair(deep[n]))
                )
            out_ref[s, 48:56, :] = jnp.concatenate(
                [speed[0][0:1], speed[1][0:1], speed[0][15:16], speed[1][15:16]] + [zero_row] * 4,
                axis=0,
            )


def load_kernel(source_ref, _, along_ref, cross_ref, deep_ref, force_ref, to_low_ref, to_high_ref, sem):
    snaps, layers = force_ref.shape[:2]
    fields = (along_ref, cross_ref, deep_ref)
    copies = [
        pltpu.make_async_copy(source_ref.at[n], fields[n % 3].at[n // 3], sem.at[n]) for n in range(3 * snaps)
    ]
    for copy in copies:
        copy.start()
    for s in range(snaps):
        for copy in copies[3 * s : 3 * s + 3]:
            copy.wait()
        for i in range(layers):
            along = 0.0
            if i < layers - 1:
                along = along + along_ref[s, i + 1]
            if i > 0:
                along = along - along_ref[s, i - 1]
            cross = row_pair(cross_ref[s, i], 0.0, 0.0)
            force_ref[s, i] = -0.5 * (
                along + difference(cross) + difference(depth_pair(deep_ref[s, i]))
            )
        for out_ref, layer, second in ((to_low_ref, 0, 1), (to_high_ref, layers - 1, layers - 2)):
            out_ref[s, 0:32, :] = force_ref[s, second]
            out_ref[s, 32:64, :] = force_ref[s, layer]
            out_ref[s, 64:96, :] = along_ref[s, layer]


def fix_kernel(cross_ref, force_ref, from_low_ref, from_high_ref, to_low_ref, to_high_ref):
    layers = force_ref.shape[1]
    keep_low, keep_high = inside("ana")
    for s in range(to_low_ref.shape[0]):
        for out_ref, layer, second, pillar in ((to_low_ref, 0, 1, 48), (to_high_ref, layers - 1, layers - 2, 50)):

            def halo(side_ref, keep, row):
                return jnp.where(keep, side_ref[s, row : row + 1, :], 0.0)

            cross = cross_ref[s, layer]
            row = 16 + layer
            below = jnp.where(keep_low, from_low_ref[s, row : row + 1, :] - 0.5 * cross[0:1], 0.0)
            above = jnp.where(keep_high, from_high_ref[s, row : row + 1, :] + 0.5 * cross[31:32], 0.0)
            rows = [
                force_ref[s, layer, 0:1, :] + 0.5 * halo(from_low_ref, keep_low, layer),
                force_ref[s, layer, 31:32, :] - 0.5 * halo(from_high_ref, keep_high, layer),
                force_ref[s, second, 0:1, :] + 0.5 * halo(from_low_ref, keep_low, second),
                force_ref[s, second, 31:32, :] - 0.5 * halo(from_high_ref, keep_high, second),
                halo(from_low_ref, keep_low, pillar + 1),
                halo(from_low_ref, keep_low, pillar),
                halo(from_high_ref, keep_high, pillar),
                halo(from_high_ref, keep_high, pillar + 1),
                below,
                above,
            ]
            rows = rows + [jnp.zeros_like(below)] * (FIX_ROWS - len(rows))
            out_ref[s] = jnp.concatenate(rows, axis=0)


def sample_layers(s, parts, layers, fields, owner, weight_ref, pool_ref, out_ref, split_ref, pooled_ref, press, beside):
    count = len(layers)
    for n, i in enumerate(layers):
        centre = press(i)
        after_row, before_row = beside(i)
        gradient = (
            press(i + 1) - press(i - 1),
            difference(row_pair(centre, after_row, before_row)),
            difference(depth_pair(centre)),
        )
        weight = weight_ref[32 * i : 32 * i + 32, :]
        for c in range(3):
            kept = (fields[c][s, i] - 0.5 * gradient[c]) * weight
            row = 32 * (c * count + n)
            for p in range(parts):
                piece = kept.astype(jnp.bfloat16)
                split_ref[row : row + 32, 256 * p : 256 * p + 256] = piece
                if p < parts - 1:
                    kept = kept - piece.astype(jnp.float32)
    pooled = jnp.dot(split_ref[...], pool_ref[...], preferred_element_type=jnp.float32)
    pooled_ref[0] = pooled[:, :LANES]
    pooled_ref[1] = pooled[:, LANES:]
    rows = 3 * count * 32
    flat = pooled_ref.reshape(2 * rows, LANES)
    out_flat = out_ref.reshape(out_ref.shape[0] * 3 * 32, LANES)
    for n, i in enumerate(layers):
        for half in range(2):
            place = owner(2 * i + half)
            for c in range(3):
                start = 32 * (c * count + n) + 16 * half
                tile = flat[pl.ds(start, 8, stride=2), :] + flat[pl.ds(start + rows + 1, 8, stride=2), :]
                out_flat[pl.ds((place * 3 + c) * 32 + s, 8, stride=4), :] = tile


def inner_kernel(
    parts, owner_ref, along_ref, cross_ref, deep_ref, own_force_ref, weight_ref, pool_ref, low_ref, high_ref,
    force_ref, press_ref, out_ref, side_ref, split_ref, pooled_ref,
):
    layers = along_ref.shape[1]
    keep_low, keep_high = inside("ana")
    brick = lax.axis_index("brick")

    def snapshot(s, carry):
        def halo(ref, keep, start, size=1):
            return jnp.where(keep, ref[s, start : start + size, :], 0.0)

        row_at = lax.broadcasted_iota(jnp.int32, (8, along_ref.shape[3]), 0)
        for i in range(layers):
            first, last = own_force_ref[s, i, 0:8, :], own_force_ref[s, i, 24:32, :]
            force_ref[s, i, 0:8, :] = jnp.where(row_at == 0, first + 0.5 * halo(low_ref, keep_low, i), first)
            force_ref[s, i, 8:24, :] = own_force_ref[s, i, 8:24, :]
            force_ref[s, i, 24:32, :] = jnp.where(row_at == 7, last - 0.5 * halo(high_ref, keep_high, i), last)

        for side, ref, keep, row, sign in ((0, low_ref, keep_low, 0, -0.5), (1, high_ref, keep_high, 31, 0.5)):
            own_cross = jnp.concatenate([cross_ref[s, i, row : row + 1, :] for i in range(layers)], axis=0)
            own_force = jnp.concatenate([force_ref[s, i, row : row + 1, :] for i in range(layers)], axis=0)
            edge = ref[s, 16:32, :] + sign * own_cross
            zero_row = jnp.zeros((1, edge.shape[1]), jnp.float32)
            around = sum(row_pair(edge, zero_row, zero_row)) + ref[s, 32:48, :] + own_force
            around = around + sum(depth_pair(edge))
            side_ref[2 + side] = jnp.where(keep, edge, 0.0)
            side_ref[side] = jnp.where(keep, relaxed(edge, around), 0.0)

        for i in range(MARGIN - 1, layers - MARGIN + 1):
            field = force_ref[s, i]
            beside = row_pair(field, side_ref[3, i : i + 1, :], side_ref[2, i : i + 1, :])
            around = (force_ref[s, i + 1] + force_ref[s, i - 1]) + sum(beside) + sum(depth_pair(field))
            press_ref[s, i] = relaxed(field, around)

        sample_layers(
            s, parts, list(range(MARGIN, layers - MARGIN)), (along_ref, cross_ref, deep_ref),
            lambda k: owner_ref[brick, k], weight_ref, pool_ref,
            out_ref, split_ref, pooled_ref,
            lambda i: press_ref[s, i],
            lambda i: (side_ref[1, i : i + 1, :], side_ref[0, i : i + 1, :]),
        )
        return carry

    lax.fori_loop(0, along_ref.shape[0], snapshot, 0)


def outer_kernel(
    parts, owner_ref, along_ref, cross_ref, deep_ref, weight_ref, pool_ref, low_ref, high_ref, before_ref, after_ref,
    before_fix_ref, after_fix_ref, inner_force_ref, inner_press_ref, _, out_ref, force_ref, press_ref, side_force_ref, side_press_ref,
    split_ref, pooled_ref,
):
    layers = along_ref.shape[1]
    keep_before, keep_after = inside("brick")
    keep_low, keep_high = inside("ana")
    brick = lax.axis_index("brick")

    def snapshot(s, carry):
        def halo(ref, keep, start, size=1):
            return jnp.where(keep, ref[s, start : start + size, :], 0.0)

        def fixed(ref, fix_ref, start, row):
            field = ref[s, start : start + 32, :]
            row_at = lax.broadcasted_iota(jnp.int32, field.shape, 0)
            field = jnp.where(row_at == 0, fix_ref[s, row : row + 1, :], field)
            return jnp.where(row_at == 31, fix_ref[s, row + 1 : row + 2, :], field)

        first, last = along_ref[s, 0], along_ref[s, layers - 1]
        force_ref[0] = jnp.where(keep_before, fixed(before_ref, before_fix_ref, 0, 2), 0.0)
        force_ref[1] = jnp.where(keep_before, fixed(before_ref, before_fix_ref, 32, 0) - 0.5 * first, 0.0)
        force_ref[2] = inner_force_ref[s, 0] + 0.5 * halo(before_ref, keep_before, 64, 32)
        force_ref[3] = inner_force_ref[s, layers - 1] - 0.5 * halo(after_ref, keep_after, 64, 32)
        force_ref[4] = jnp.where(keep_after, fixed(after_ref, after_fix_ref, 32, 0) + 0.5 * last, 0.0)
        force_ref[5] = jnp.where(keep_after, fixed(after_ref, after_fix_ref, 0, 2), 0.0)

        def force(i):
            if i < 1:
                return force_ref[i + 2]
            if i > layers - 2:
                return force_ref[i - layers + 4]
            return inner_force_ref[s, i]

        for side, ref, keep, far, near, corner, row, sign in (
            (0, low_ref, keep_low, 4, 5, 8, 0, -0.5),
            (1, high_ref, keep_high, 7, 6, 9, 31, 0.5),
        ):
            own_cross = jnp.concatenate([cross_ref[s, i, row : row + 1, :] for i in range(layers)], axis=0)
            own_force = jnp.concatenate(
                [force_ref[2, row : row + 1, :]]
                + [inner_force_ref[s, i, row : row + 1, :] for i in range(1, layers - 1)]
                + [force_ref[3, row : row + 1, :]],
                axis=0,
            )
            row_at = lax.broadcasted_iota(jnp.int32, own_force.shape, 0)

            def ends(at):
                first = 0.5 * halo(before_fix_ref, keep_before, at)
                last = -0.5 * halo(after_fix_ref, keep_after, at)
                return jnp.where(row_at == 0, first, 0.0) + jnp.where(row_at == layers - 1, last, 0.0)

            edge = jnp.where(keep, ref[s, 16:32, :] + sign * own_cross + ends(near), 0.0)
            beyond = jnp.where(keep, ref[s, 32:48, :] + ends(far), 0.0)
            corner_before = jnp.where(keep_before, halo(before_fix_ref, keep, corner) - 0.5 * halo(ref, keep, 48), 0.0)
            corner_after = jnp.where(keep_after, halo(after_fix_ref, keep, corner) + 0.5 * halo(ref, keep, 50), 0.0)
            around = sum(row_pair(edge, corner_after, corner_before)) + beyond + own_force
            around = around + sum(depth_pair(edge))
            side_press_ref[side] = jnp.where(keep, relaxed(edge, around), 0.0)
            side_force_ref[side, 8:24, :] = edge
            side_force_ref[side, 7:8, :] = corner_before
            side_force_ref[side, 24:25, :] = corner_after

        low_layers, high_layers = list(range(-1, MARGIN - 1)), list(range(layers - MARGIN + 1, layers + 1))
        place = {i: n for n, i in enumerate(low_layers + high_layers)}
        for i in place:
            field = force(i)
            beside = row_pair(field, side_force_ref[1, 8 + i : 9 + i, :], side_force_ref[0, 8 + i : 9 + i, :])
            around = (force(i + 1) + force(i - 1)) + sum(beside) + sum(depth_pair(field))
            press = relaxed(field, around)
            if i == -1:
                press = jnp.where(keep_before, press, 0.0)
            if i == layers:
                press = jnp.where(keep_after, press, 0.0)
            press_ref[place[i]] = press

        sample_layers(
            s, parts, list(range(MARGIN)) + list(range(layers - MARGIN, layers)), (along_ref, cross_ref, deep_ref),
            lambda k: owner_ref[brick, k], weight_ref, pool_ref, out_ref, split_ref, pooled_ref,
            lambda i: press_ref[place[i]] if i in place else inner_press_ref[s, i],
            lambda i: (side_press_ref[1, i : i + 1, :], side_press_ref[0, i : i + 1, :]),
        )
        return carry

    lax.fori_loop(0, along_ref.shape[0], snapshot, 0)


def weight_kernel(parts, index_ref, out_ref, pool_ref, wide_ref):
    pool_ref[...] = pooling(parts)
    rows = index_ref.shape[0]
    at = lax.broadcasted_iota(jnp.int32, (rows, LANES), 0) * LANES + lax.broadcasted_iota(jnp.int32, (rows, LANES), 1)
    offset = (index_ref[...] - 4 * at).astype(jnp.float32).astype(jnp.bfloat16)
    source = lax.broadcasted_iota(jnp.int32, (LANES, 512), 0)
    target = lax.broadcasted_iota(jnp.int32, (LANES, 512), 1)
    expand = jnp.where(target // 4 == source, 1.0, 0.0).astype(jnp.bfloat16)
    wide = jnp.dot(offset, expand, preferred_element_type=jnp.float32)
    lane_at = lax.broadcasted_iota(jnp.int32, wide.shape, 1)
    hit = jnp.where(wide == (lane_at % 4).astype(jnp.float32), 1.0, 0.0)
    for half in range(2):
        for kt in range(2):
            wide_ref[kt, pl.ds(half, rows, stride=2), :] = hit[:, 256 * half + 128 * kt : 256 * half + 128 * kt + 128]
    for kt in range(2):
        out_ref[:, 128 * kt : 128 * kt + 128] = wide_ref[kt]


def pooling(parts):
    source = lax.broadcasted_iota(jnp.int32, (256 * parts, 256), 0) % 256
    target = lax.broadcasted_iota(jnp.int32, (256 * parts, 256), 1)
    low = (target < 64) & (source // 4 == target)
    high = (target >= 192) & (source // 4 == target - 192)
    return jnp.where(low | high, 1.0, 0.0).astype(jnp.bfloat16)


def exchange(to_before, to_after, axis):
    devices = lax.axis_size(axis)
    up = [(i, (i + 1) % devices) for i in range(devices)]
    down = [(j, i) for i, j in up]
    return lax.ppermute(to_after, axis, up), lax.ppermute(to_before, axis, down)


def grid_kernel(kernel, name, cost, **kwargs):
    flops, data = cost
    return pl.pallas_call(
        kernel,
        compiler_params=pltpu.CompilerParams(vmem_limit_bytes=VMEM_LIMIT),
        cost_estimate=pl.CostEstimate(flops=flops, bytes_accessed=data, transcendentals=0),
        name=name,
        **kwargs,
    )


def front(provisional, sample_index, owner_table):
    snaps, comps, layers, columns, depth = provisional.shape
    bricks = lax.axis_size("brick")
    smem = pl.BlockSpec(memory_space=pltpu.SMEM)
    vmem = pl.BlockSpec(memory_space=pltpu.VMEM)
    samples = layers * columns * depth // 4
    source = provisional.reshape(snaps * comps, layers, columns, depth)
    f32 = lambda *shape: jax.ShapeDtypeStruct(shape, jnp.float32)
    scratch = lambda *shape: pltpu.VMEM(shape, jnp.float32)

    tiles = source.reshape(snaps * comps, layers, columns // 8, 8, 2, LANES)
    tiles = tiles.transpose(0, 1, 2, 4, 3, 5).reshape(snaps * comps, layers, columns // 8, 16, LANES)
    to_low, to_high = grid_kernel(
        ana_edge_kernel,
        "ana_edges",
        (10**6, 4 * 10**6),
        in_specs=[pl.BlockSpec(memory_space=pltpu.HBM)],
        out_specs=[vmem] * 2,
        out_shape=[f32(snaps, ANA_ROWS, depth)] * 2,
        scratch_shapes=[scratch(snaps * comps, layers, 16, LANES)] * 2 + [pltpu.SemaphoreType.DMA((2,))],
    )(pltpu.with_memory_space_constraint(tiles, pltpu.HBM))
    from_low, from_high = exchange(to_low, to_high, "ana")

    weight, pool = grid_kernel(
        functools.partial(weight_kernel, POOL_PARTS),
        "weights",
        (10**6, 10**6),
        in_specs=[vmem],
        out_specs=[vmem] * 2,
        out_shape=[f32(layers * columns, depth), jax.ShapeDtypeStruct((256 * POOL_PARTS, 256), jnp.bfloat16)],
        scratch_shapes=[scratch(2, layers * columns, LANES)],
    )(sample_index.reshape(samples // LANES, LANES))

    *fields, own_force, to_before, to_after = grid_kernel(
        load_kernel,
        "load",
        (10**8, 6 * 10**6),
        in_specs=[pl.BlockSpec(memory_space=pltpu.HBM), pl.BlockSpec(memory_space=pl.ANY)],
        out_specs=[vmem] * 6,
        out_shape=[f32(snaps, layers, columns, depth)] * 4 + [f32(snaps, BULK_ROWS, depth)] * 2,
        scratch_shapes=[pltpu.SemaphoreType.DMA((snaps * comps,))],
    )(pltpu.with_memory_space_constraint(source, pltpu.HBM), to_low)
    from_before, from_after = exchange(to_before, to_after, "brick")

    to_before, to_after = grid_kernel(
        fix_kernel,
        "fix",
        (10**5, 10**6),
        in_specs=[vmem] * 4,
        out_specs=[vmem] * 2,
        out_shape=[f32(snaps, FIX_ROWS, depth)] * 2,
    )(fields[1], own_force, from_low, from_high)
    before_fix, after_fix = exchange(to_before, to_after, "brick")

    split_shape = lambda count: pltpu.VMEM((3 * 32 * count, 256 * POOL_PARTS), jnp.bfloat16)
    force, press, outgoing = grid_kernel(
        functools.partial(inner_kernel, POOL_PARTS),
        "inner_layers",
        (4 * 10**9, 2 * 10**7),
        in_specs=[smem] + [vmem] * 8,
        out_specs=[vmem] * 3,
        out_shape=[f32(snaps, layers, columns, depth)] * 2 + [f32(bricks, comps, 32, LANES)],
        scratch_shapes=[
            scratch(4, layers, depth),
            split_shape(layers - 2 * MARGIN),
            scratch(2, 3 * 32 * (layers - 2 * MARGIN), LANES),
        ],
    )(owner_table, *fields, own_force, weight, pool, from_low, from_high)
    return grid_kernel(
        functools.partial(outer_kernel, POOL_PARTS),
        "outer_layers",
        (3 * 10**9, 10**7),
        in_specs=[smem] + [vmem] * 14,
        out_specs=vmem,
        out_shape=f32(bricks, comps, 32, LANES),
        scratch_shapes=[
            scratch(6, columns, depth),
            scratch(2 * MARGIN, columns, depth),
            scratch(2, 32, depth),
            scratch(2, layers, depth),
            split_shape(2 * MARGIN),
            scratch(2, 3 * 32 * 2 * MARGIN, LANES),
        ],
        input_output_aliases={14: 0},
    )(owner_table, *fields, weight, pool, from_low, from_high, from_before, from_after, before_fix, after_fix, force, press, outgoing)


def per_device(provisional, sample_index, owner_table, weighted_basis):
    snaps = provisional.shape[0]
    rank_count = weighted_basis.shape[0]
    devices = lax.axis_size("brick") * lax.axis_size("ana")
    total_rows = 3.0 * sample_index.shape[2] * devices
    outgoing = front(provisional, sample_index, owner_table)
    arrived = lax.all_to_all(outgoing, "brick", split_axis=0, concat_axis=0, tiled=True)
    basis = jnp.transpose(weighted_basis, (1, 0, 2))
    new_basis, core = tail(basis, arrived, WIDTH, total_rows, devices)
    count = rank_count + snaps
    return (jnp.transpose(new_basis, (1, 0, 2)), core[:count, :count])


def solution(mesh):
    placed = (
        P(None, None, "brick", "ana", None),
        P("brick", "ana", None),
        P(),
        P(None, None, ("brick", "ana")),
    )
    return jax.shard_map(
        per_device,
        mesh=mesh,
        in_specs=placed,
        out_specs=(P(None, None, ("brick", "ana")), P()),
        check_vma=False,
    )
```

```python
import functools
import jax
import jax.numpy as jnp
from jax import lax
from jax.experimental import pallas as pl
from jax.experimental.pallas import tpu as pltpu
from jax.sharding import PartitionSpec as P

LANES = 128
PACK = 24
GRAM = 20
POOL_PARTS = 2
WIDTH = 8192
SLOTS = 4
VMEM_LIMIT = 20 * 1024 * 1024


def split_pieces(block):
    high = block.astype(jnp.bfloat16)
    return high, (block - high.astype(jnp.float32)).astype(jnp.bfloat16)


def sample_pieces(arrived_ref, c, start, width):
    at = lax.broadcasted_iota(jnp.int32, (8, LANES), 0)
    tiles = []
    for b in range(start // 1024, (start + width) // 1024):
        for n in range(0, 32, 8):
            both = arrived_ref[b, c, n : n + 8, :]
            high = both.astype(jnp.bfloat16).astype(jnp.float32)
            low = both - high
            tiles.append(jnp.where(at < 4, high, pltpu.roll(low, 4, 0)))
            tiles.append(jnp.where(at < 4, pltpu.roll(high, 4, 0), low))
    rows = jnp.concatenate(tiles, axis=1)
    return jnp.concatenate([rows, rows], axis=0).astype(jnp.bfloat16)


def stacked_pieces(basis_ref, arrived_ref, c, start, width, order):
    large = split_pieces(basis_ref[c, :, start : start + width])
    return jnp.concatenate([large[p] for p in order] + [sample_pieces(arrived_ref, c, start, width)], axis=0)


def gram_kernel(width, scale, basis_ref, arrived_ref, out_ref):
    comps, rank_count, columns = basis_ref.shape
    total = 0.0
    for c in range(comps):
        for start in range(0, columns, width):
            pieces = stacked_pieces(basis_ref, arrived_ref, c, start, width, (0, 1))
            total = total + lax.dot_general(
                pieces, pieces, (((1,), (1,)), ((), ())), preferred_element_type=jnp.float32
            )
    total = jnp.concatenate([total, jnp.zeros((total.shape[0], LANES - total.shape[1]), jnp.float32)], axis=1)
    lane_at = lax.broadcasted_iota(jnp.int32, total.shape, 1)
    left = jnp.where(lane_at < 16, total, pltpu.roll(total, LANES - 20, 1)) + pltpu.roll(total, LANES - 16, 1)
    left = jnp.where(lane_at < GRAM, left, 0.0) * scale
    row_at = lax.broadcasted_iota(jnp.int32, (8, LANES), 0)
    small = jnp.where(row_at < 4, left[32:40] + pltpu.roll(left[32:40], 4, 0), 0.0)
    packed = left[0:8] + left[16:24]
    packed = packed + pltpu.roll(left[8:16] + left[24:32], GRAM, 1) + pltpu.roll(small, 2 * GRAM, 1)
    packed = packed[0:4] + pltpu.roll(packed, 3 * GRAM, 1)[4:8]
    out_ref[...] = jnp.broadcast_to(packed[None], out_ref.shape)


def factor(tiles, count, block):
    row_at = [lax.broadcasted_iota(jnp.int32, (8, LANES), 0) + 8 * t for t in range(3)]
    lane_at = lax.broadcasted_iota(jnp.int32, (8, LANES), 1)
    work = [jnp.where(lane_at < PACK, tiles[t], 0.0) + jnp.where(lane_at == row_at[t] + 32, 1.0, 0.0) for t in range(3)]
    diagonal = [jnp.ones((8, LANES), jnp.float32)] * 3

    def spread(piece):
        return jnp.broadcast_to(piece, (8, LANES))

    for j in range(0, count, block):
        later = [t for t in range(3) if j + block < count and 8 * t + 8 > j + block]
        rows = [spread(work[(j + q) // 8][(j + q) % 8 : (j + q) % 8 + 1]) for q in range(block)]
        cols = [{t: spread(work[t][:, j + q : j + q + 1]) for t in later} for q in range(block)]
        pivots = [[spread(rows[q][:, j + r : j + r + 1]) if r >= q else None for r in range(block)] for q in range(block)]
        for q in range(block):
            inverse = 1.0 / pivots[q][q]
            for r in range(q + 1, block):
                ratio = pivots[q][r] * inverse
                rows[r] = rows[r] - ratio * rows[q]
                for t in later:
                    cols[r][t] = cols[r][t] - ratio * cols[q][t]
                for u in range(r, block):
                    pivots[r][u] = pivots[r][u] - ratio * pivots[q][u]
            for t in later:
                ratio = jnp.where(row_at[t] >= j + block, cols[q][t] * inverse, 0.0)
                work[t] = work[t] - ratio * rows[q]
            t = (j + q) // 8
            work[t] = jnp.where(row_at[t] == j + q, rows[q], work[t])
            diagonal[t] = jnp.where(row_at[t] == j + q, pivots[q][q], diagonal[t])
    work = [work[t] / jnp.sqrt(diagonal[t]) for t in range(3)]
    upper = [jnp.where((lane_at >= row_at[t]) & (lane_at < PACK), work[t], 0.0) for t in range(3)]
    inverse = jnp.concatenate([pltpu.roll(work[t], LANES - 32, 1)[:, :PACK] for t in range(3)], axis=0)
    return upper, inverse


def apply_kernel(width, slots, basis_ref, arrived_ref, packed_ref, out_ref, core_ref, left_ref, slot_ref, sem):
    comps, rank_count, columns = basis_ref.shape
    count = out_ref.shape[1]
    packed = jnp.sum(packed_ref[...], axis=0)
    packed = jnp.concatenate([packed, pltpu.roll(packed, LANES - 3 * GRAM, 1)], axis=0)
    lane_at = lax.broadcasted_iota(jnp.int32, packed.shape, 1)
    tiles = [packed, pltpu.roll(packed, LANES - GRAM, 1), pltpu.roll(packed, LANES - 2 * GRAM, 1)]
    tiles = [jnp.where(lane_at < GRAM, tile, 0.0) for tile in tiles]
    upper, inverse = factor(tiles, count, count // 2)
    for t in range(3):
        core_ref[8 * t : 8 * t + 8, :] = upper[t]
    high, low = [piece.astype(jnp.float32) for piece in split_pieces(inverse)]
    order = (high, high, low)
    left = [piece[:, :rank_count] for piece in order] + [piece[:, rank_count:count] for piece in order]
    left.append(jnp.zeros((PACK, 16 - 4 * len(order)), jnp.float32))
    left_ref[...] = jnp.concatenate(left, axis=1).astype(jnp.bfloat16)

    blocks = [(c, start) for c in range(comps) for start in range(0, columns, width)]
    copies = []
    for n, (c, start) in enumerate(blocks):
        if n >= slots:
            copies[n - slots].wait()
        pieces = stacked_pieces(basis_ref, arrived_ref, c, start, width, (0, 1, 0))
        product = jnp.dot(left_ref[...], pieces, preferred_element_type=jnp.float32)
        slot = n % slots
        slot_ref[slot] = product[:count]
        copy = pltpu.make_async_copy(slot_ref.at[slot], out_ref.at[c, :, start : start + width], sem.at[slot])
        copy.start()
        copies.append(copy)
    for copy in copies[-slots:]:
        copy.wait()


def tail(basis, arrived, width, total_rows, devices):
    comps, rank_count, rows = basis.shape
    vmem = pl.BlockSpec(memory_space=pltpu.VMEM)
    copies = grid_kernel(
        functools.partial(gram_kernel, width, 1.0 / total_rows),
        "gram",
        (10**9, 10**7),
        in_specs=[vmem, vmem],
        out_specs=vmem,
        out_shape=jax.ShapeDtypeStruct((devices, 4, LANES), jnp.float32),
    )(basis, arrived)
    partial_sums = lax.all_to_all(copies, ("brick", "ana"), 0, 0, tiled=True)
    count = rank_count + 4
    return grid_kernel(
        functools.partial(apply_kernel, width, SLOTS),
        "apply",
        (10**9, 2 * 10**7),
        in_specs=[vmem] * 3,
        out_specs=[pl.BlockSpec(memory_space=pltpu.HBM), vmem],
        out_shape=[
            jax.ShapeDtypeStruct((comps, count, rows), jnp.float32),
            jax.ShapeDtypeStruct((PACK, LANES), jnp.float32),
        ],
        scratch_shapes=[
            pltpu.VMEM((PACK, rank_count * 3 + 16), jnp.bfloat16),
            pltpu.VMEM((SLOTS, count, width), jnp.float32),
            pltpu.SemaphoreType.DMA((SLOTS,)),
        ],
    )(basis, arrived, partial_sums)


ANA_ROWS = 56
BULK_ROWS = 96
FIX_ROWS = 16
MARGIN = 3


def depth_pair(field):
    lanes = field.shape[-1]
    lane_at = lax.broadcasted_iota(jnp.int32, field.shape, field.ndim - 1)
    after = jnp.where(lane_at == lanes - 1, 0.0, pltpu.roll(field, lanes - 1, field.ndim - 1))
    before = jnp.where(lane_at == 0, 0.0, pltpu.roll(field, 1, field.ndim - 1))
    return after, before


def row_pair(field, after_row, before_row):
    rows = field.shape[0]
    row_at = lax.broadcasted_iota(jnp.int32, field.shape, 0)
    after = jnp.where(row_at == rows - 1, after_row, pltpu.roll(field, rows - 1, 0))
    before = jnp.where(row_at == 0, before_row, pltpu.roll(field, 1, 0))
    return after, before


def inside(axis):
    at = lax.axis_index(axis)
    return at > 0, at < lax.axis_size(axis) - 1


def difference(pair):
    return pair[0] - pair[1]


def relaxed(field, around):
    return (field + around * (1.0 / 6.0)) * (1.0 / 6.0)


def ana_edge_kernel(tiles_ref, to_low_ref, to_high_ref, low_ref, high_ref, sem):
    snaps = to_low_ref.shape[0]
    fields, layers, rows, lanes = low_ref.shape
    last = tiles_ref.shape[2] - 1
    copies = []
    for s in range(snaps):
        span = pl.ds(3 * s, 3)
        for n, (at, ref) in enumerate(((0, low_ref), (last, high_ref))):
            copies.append(pltpu.make_async_copy(tiles_ref.at[span, :, at], ref.at[span], sem.at[2 * s + n]))
    for copy in copies:
        copy.start()
    flat = (fields * layers * rows, lanes)

    def column(ref, s, c, j):
        start = (s * 3 + c) * layers * rows + j
        return jnp.concatenate(
            [ref[pl.ds(start + 8 * half, layers, stride=rows), :] for half in range(2)], axis=1
        )

    zero_row = jnp.zeros((1, 2 * lanes), jnp.float32)
    for s in range(snaps):
        for n, (side_ref, out_ref, edge, second, third, sign) in enumerate(
            ((low_ref, to_low_ref, 0, 1, 2, 1.0), (high_ref, to_high_ref, 7, 6, 5, -1.0))
        ):
            copies[2 * s + n].wait()
            ref = side_ref.reshape(*flat)
            speed = [column(ref, s, 0, j) for j in (edge, second)]
            cross = [column(ref, s, 1, j) for j in (edge, second, third)]
            deep = [column(ref, s, 2, j) for j in (edge, second)]
            beside = (sign * cross[1], sign * (cross[2] - cross[0]))
            out_ref[s, 0:16, :] = cross[0]
            for n in range(2):
                along = difference(row_pair(speed[n], zero_row, zero_row))
                out_ref[s, 16 + 16 * n : 32 + 16 * n, :] = -0.5 * (
                    along + beside[n] + difference(depth_pair(deep[n]))
                )
            out_ref[s, 48:56, :] = jnp.concatenate(
                [speed[0][0:1], speed[1][0:1], speed[0][15:16], speed[1][15:16]] + [zero_row] * 4,
                axis=0,
            )


def load_kernel(source_ref, _, along_ref, cross_ref, deep_ref, force_ref, to_low_ref, to_high_ref, sem):
    snaps, layers = force_ref.shape[:2]
    fields = (along_ref, cross_ref, deep_ref)
    copies = [
        pltpu.make_async_copy(source_ref.at[n], fields[n % 3].at[n // 3], sem.at[n]) for n in range(3 * snaps)
    ]
    for copy in copies:
        copy.start()
    for s in range(snaps):
        for copy in copies[3 * s : 3 * s + 3]:
            copy.wait()
        for i in range(layers):
            along = 0.0
            if i < layers - 1:
                along = along + along_ref[s, i + 1]
            if i > 0:
                along = along - along_ref[s, i - 1]
            cross = row_pair(cross_ref[s, i], 0.0, 0.0)
            force_ref[s, i] = -0.5 * (
                along + difference(cross) + difference(depth_pair(deep_ref[s, i]))
            )
        for out_ref, layer, second in ((to_low_ref, 0, 1), (to_high_ref, layers - 1, layers - 2)):
            out_ref[s, 0:32, :] = force_ref[s, second]
            out_ref[s, 32:64, :] = force_ref[s, layer]
            out_ref[s, 64:96, :] = along_ref[s, layer]


def fix_kernel(cross_ref, force_ref, from_low_ref, from_high_ref, to_low_ref, to_high_ref):
    layers = force_ref.shape[1]
    keep_low, keep_high = inside("ana")
    for s in range(to_low_ref.shape[0]):
        for out_ref, layer, second, pillar in ((to_low_ref, 0, 1, 48), (to_high_ref, layers - 1, layers - 2, 50)):

            def halo(side_ref, keep, row):
                return jnp.where(keep, side_ref[s, row : row + 1, :], 0.0)

            cross = cross_ref[s, layer]
            row = 16 + layer
            below = jnp.where(keep_low, from_low_ref[s, row : row + 1, :] - 0.5 * cross[0:1], 0.0)
            above = jnp.where(keep_high, from_high_ref[s, row : row + 1, :] + 0.5 * cross[31:32], 0.0)
            rows = [
                force_ref[s, layer, 0:1, :] + 0.5 * halo(from_low_ref, keep_low, layer),
                force_ref[s, layer, 31:32, :] - 0.5 * halo(from_high_ref, keep_high, layer),
                force_ref[s, second, 0:1, :] + 0.5 * halo(from_low_ref, keep_low, second),
                force_ref[s, second, 31:32, :] - 0.5 * halo(from_high_ref, keep_high, second),
                halo(from_low_ref, keep_low, pillar + 1),
                halo(from_low_ref, keep_low, pillar),
                halo(from_high_ref, keep_high, pillar),
                halo(from_high_ref, keep_high, pillar + 1),
                below,
                above,
            ]
            rows = rows + [jnp.zeros_like(below)] * (FIX_ROWS - len(rows))
            out_ref[s] = jnp.concatenate(rows, axis=0)


def sample_layers(s, parts, layers, fields, owner, weight_ref, pool_ref, out_ref, split_ref, pooled_ref, press, beside):
    count = len(layers)
    for n, i in enumerate(layers):
        centre = press(i)
        after_row, before_row = beside(i)
        gradient = (
            press(i + 1) - press(i - 1),
            difference(row_pair(centre, after_row, before_row)),
            difference(depth_pair(centre)),
        )
        weight = weight_ref[32 * i : 32 * i + 32, :]
        for c in range(3):
            kept = (fields[c][s, i] - 0.5 * gradient[c]) * weight
            row = 32 * (c * count + n)
            for p in range(parts):
                piece = kept.astype(jnp.bfloat16)
                split_ref[row : row + 32, 256 * p : 256 * p + 256] = piece
                if p < parts - 1:
                    kept = kept - piece.astype(jnp.float32)
    pooled = jnp.dot(split_ref[...], pool_ref[...], preferred_element_type=jnp.float32)
    pooled_ref[0] = pooled[:, :LANES]
    pooled_ref[1] = pooled[:, LANES:]
    rows = 3 * count * 32
    flat = pooled_ref.reshape(2 * rows, LANES)
    out_flat = out_ref.reshape(out_ref.shape[0] * 3 * 32, LANES)
    for n, i in enumerate(layers):
        for half in range(2):
            place = owner(2 * i + half)
            for c in range(3):
                start = 32 * (c * count + n) + 16 * half
                tile = flat[pl.ds(start, 8, stride=2), :] + flat[pl.ds(start + rows + 1, 8, stride=2), :]
                out_flat[pl.ds((place * 3 + c) * 32 + s, 8, stride=4), :] = tile


def inner_kernel(
    parts, owner_ref, along_ref, cross_ref, deep_ref, own_force_ref, weight_ref, pool_ref, low_ref, high_ref,
    force_ref, press_ref, out_ref, side_ref, split_ref, pooled_ref,
):
    layers = along_ref.shape[1]
    keep_low, keep_high = inside("ana")
    brick = lax.axis_index("brick")

    def snapshot(s, carry):
        def halo(ref, keep, start, size=1):
            return jnp.where(keep, ref[s, start : start + size, :], 0.0)

        row_at = lax.broadcasted_iota(jnp.int32, (8, along_ref.shape[3]), 0)
        for i in range(layers):
            first, last = own_force_ref[s, i, 0:8, :], own_force_ref[s, i, 24:32, :]
            force_ref[s, i, 0:8, :] = jnp.where(row_at == 0, first + 0.5 * halo(low_ref, keep_low, i), first)
            force_ref[s, i, 8:24, :] = own_force_ref[s, i, 8:24, :]
            force_ref[s, i, 24:32, :] = jnp.where(row_at == 7, last - 0.5 * halo(high_ref, keep_high, i), last)

        for side, ref, keep, row, sign in ((0, low_ref, keep_low, 0, -0.5), (1, high_ref, keep_high, 31, 0.5)):
            own_cross = jnp.concatenate([cross_ref[s, i, row : row + 1, :] for i in range(layers)], axis=0)
            own_force = jnp.concatenate([force_ref[s, i, row : row + 1, :] for i in range(layers)], axis=0)
            edge = ref[s, 16:32, :] + sign * own_cross
            zero_row = jnp.zeros((1, edge.shape[1]), jnp.float32)
            around = sum(row_pair(edge, zero_row, zero_row)) + ref[s, 32:48, :] + own_force
            around = around + sum(depth_pair(edge))
            side_ref[2 + side] = jnp.where(keep, edge, 0.0)
            side_ref[side] = jnp.where(keep, relaxed(edge, around), 0.0)

        for i in range(MARGIN - 1, layers - MARGIN + 1):
            field = force_ref[s, i]
            beside = row_pair(field, side_ref[3, i : i + 1, :], side_ref[2, i : i + 1, :])
            around = (force_ref[s, i + 1] + force_ref[s, i - 1]) + sum(beside) + sum(depth_pair(field))
            press_ref[s, i] = relaxed(field, around)

        sample_layers(
            s, parts, list(range(MARGIN, layers - MARGIN)), (along_ref, cross_ref, deep_ref),
            lambda k: owner_ref[brick, k], weight_ref, pool_ref,
            out_ref, split_ref, pooled_ref,
            lambda i: press_ref[s, i],
            lambda i: (side_ref[1, i : i + 1, :], side_ref[0, i : i + 1, :]),
        )
        return carry

    lax.fori_loop(0, along_ref.shape[0], snapshot, 0)


def outer_kernel(
    parts, owner_ref, along_ref, cross_ref, deep_ref, weight_ref, pool_ref, low_ref, high_ref, before_ref, after_ref,
    before_fix_ref, after_fix_ref, inner_force_ref, inner_press_ref, _, out_ref, force_ref, press_ref, side_force_ref, side_press_ref,
    split_ref, pooled_ref,
):
    layers = along_ref.shape[1]
    keep_before, keep_after = inside("brick")
    keep_low, keep_high = inside("ana")
    brick = lax.axis_index("brick")

    def snapshot(s, carry):
        def halo(ref, keep, start, size=1):
            return jnp.where(keep, ref[s, start : start + size, :], 0.0)

        def fixed(ref, fix_ref, start, row):
            field = ref[s, start : start + 32, :]
            row_at = lax.broadcasted_iota(jnp.int32, field.shape, 0)
            field = jnp.where(row_at == 0, fix_ref[s, row : row + 1, :], field)
            return jnp.where(row_at == 31, fix_ref[s, row + 1 : row + 2, :], field)

        first, last = along_ref[s, 0], along_ref[s, layers - 1]
        force_ref[0] = jnp.where(keep_before, fixed(before_ref, before_fix_ref, 0, 2), 0.0)
        force_ref[1] = jnp.where(keep_before, fixed(before_ref, before_fix_ref, 32, 0) - 0.5 * first, 0.0)
        force_ref[2] = inner_force_ref[s, 0] + 0.5 * halo(before_ref, keep_before, 64, 32)
        force_ref[3] = inner_force_ref[s, layers - 1] - 0.5 * halo(after_ref, keep_after, 64, 32)
        force_ref[4] = jnp.where(keep_after, fixed(after_ref, after_fix_ref, 32, 0) + 0.5 * last, 0.0)
        force_ref[5] = jnp.where(keep_after, fixed(after_ref, after_fix_ref, 0, 2), 0.0)

        def force(i):
            if i < 1:
                return force_ref[i + 2]
            if i > layers - 2:
                return force_ref[i - layers + 4]
            return inner_force_ref[s, i]

        for side, ref, keep, far, near, corner, row, sign in (
            (0, low_ref, keep_low, 4, 5, 8, 0, -0.5),
            (1, high_ref, keep_high, 7, 6, 9, 31, 0.5),
        ):
            own_cross = jnp.concatenate([cross_ref[s, i, row : row + 1, :] for i in range(layers)], axis=0)
            own_force = jnp.concatenate(
                [force_ref[2, row : row + 1, :]]
                + [inner_force_ref[s, i, row : row + 1, :] for i in range(1, layers - 1)]
                + [force_ref[3, row : row + 1, :]],
                axis=0,
            )
            row_at = lax.broadcasted_iota(jnp.int32, own_force.shape, 0)

            def ends(at):
                first = 0.5 * halo(before_fix_ref, keep_before, at)
                last = -0.5 * halo(after_fix_ref, keep_after, at)
                return jnp.where(row_at == 0, first, 0.0) + jnp.where(row_at == layers - 1, last, 0.0)

            edge = jnp.where(keep, ref[s, 16:32, :] + sign * own_cross + ends(near), 0.0)
            beyond = jnp.where(keep, ref[s, 32:48, :] + ends(far), 0.0)
            corner_before = jnp.where(keep_before, halo(before_fix_ref, keep, corner) - 0.5 * halo(ref, keep, 48), 0.0)
            corner_after = jnp.where(keep_after, halo(after_fix_ref, keep, corner) + 0.5 * halo(ref, keep, 50), 0.0)
            around = sum(row_pair(edge, corner_after, corner_before)) + beyond + own_force
            around = around + sum(depth_pair(edge))
            side_press_ref[side] = jnp.where(keep, relaxed(edge, around), 0.0)
            side_force_ref[side, 8:24, :] = edge
            side_force_ref[side, 7:8, :] = corner_before
            side_force_ref[side, 24:25, :] = corner_after

        low_layers, high_layers = list(range(-1, MARGIN - 1)), list(range(layers - MARGIN + 1, layers + 1))
        place = {i: n for n, i in enumerate(low_layers + high_layers)}
        for i in place:
            field = force(i)
            beside = row_pair(field, side_force_ref[1, 8 + i : 9 + i, :], side_force_ref[0, 8 + i : 9 + i, :])
            around = (force(i + 1) + force(i - 1)) + sum(beside) + sum(depth_pair(field))
            press = relaxed(field, around)
            if i == -1:
                press = jnp.where(keep_before, press, 0.0)
            if i == layers:
                press = jnp.where(keep_after, press, 0.0)
            press_ref[place[i]] = press

        sample_layers(
            s, parts, list(range(MARGIN)) + list(range(layers - MARGIN, layers)), (along_ref, cross_ref, deep_ref),
            lambda k: owner_ref[brick, k], weight_ref, pool_ref, out_ref, split_ref, pooled_ref,
            lambda i: press_ref[place[i]] if i in place else inner_press_ref[s, i],
            lambda i: (side_press_ref[1, i : i + 1, :], side_press_ref[0, i : i + 1, :]),
        )
        return carry

    lax.fori_loop(0, along_ref.shape[0], snapshot, 0)


def weight_kernel(parts, index_ref, out_ref, pool_ref, wide_ref):
    pool_ref[...] = pooling(parts)
    rows = index_ref.shape[0]
    at = lax.broadcasted_iota(jnp.int32, (rows, LANES), 0) * LANES + lax.broadcasted_iota(jnp.int32, (rows, LANES), 1)
    offset = (index_ref[...] - 4 * at).astype(jnp.float32).astype(jnp.bfloat16)
    source = lax.broadcasted_iota(jnp.int32, (LANES, 512), 0)
    target = lax.broadcasted_iota(jnp.int32, (LANES, 512), 1)
    expand = jnp.where(target // 4 == source, 1.0, 0.0).astype(jnp.bfloat16)
    wide = jnp.dot(offset, expand, preferred_element_type=jnp.float32)
    lane_at = lax.broadcasted_iota(jnp.int32, wide.shape, 1)
    hit = jnp.where(wide == (lane_at % 4).astype(jnp.float32), 1.0, 0.0)
    for half in range(2):
        for kt in range(2):
            wide_ref[kt, pl.ds(half, rows, stride=2), :] = hit[:, 256 * half + 128 * kt : 256 * half + 128 * kt + 128]
    for kt in range(2):
        out_ref[:, 128 * kt : 128 * kt + 128] = wide_ref[kt]


def pooling(parts):
    source = lax.broadcasted_iota(jnp.int32, (256 * parts, 256), 0) % 256
    target = lax.broadcasted_iota(jnp.int32, (256 * parts, 256), 1)
    low = (target < 64) & (source // 4 == target)
    high = (target >= 192) & (source // 4 == target - 192)
    return jnp.where(low | high, 1.0, 0.0).astype(jnp.bfloat16)


def exchange(to_before, to_after, axis):
    devices = lax.axis_size(axis)
    up = [(i, (i + 1) % devices) for i in range(devices)]
    down = [(j, i) for i, j in up]
    return lax.ppermute(to_after, axis, up), lax.ppermute(to_before, axis, down)


def grid_kernel(kernel, name, cost, **kwargs):
    flops, data = cost
    return pl.pallas_call(
        kernel,
        compiler_params=pltpu.CompilerParams(vmem_limit_bytes=VMEM_LIMIT),
        cost_estimate=pl.CostEstimate(flops=flops, bytes_accessed=data, transcendentals=0),
        name=name,
        **kwargs,
    )


def front(provisional, sample_index, owner_table):
    snaps, comps, layers, columns, depth = provisional.shape
    bricks = lax.axis_size("brick")
    smem = pl.BlockSpec(memory_space=pltpu.SMEM)
    vmem = pl.BlockSpec(memory_space=pltpu.VMEM)
    samples = layers * columns * depth // 4
    source = provisional.reshape(snaps * comps, layers, columns, depth)
    f32 = lambda *shape: jax.ShapeDtypeStruct(shape, jnp.float32)
    scratch = lambda *shape: pltpu.VMEM(shape, jnp.float32)

    tiles = source.reshape(snaps * comps, layers, columns // 8, 8, 2, LANES)
    tiles = tiles.transpose(0, 1, 2, 4, 3, 5).reshape(snaps * comps, layers, columns // 8, 16, LANES)
    to_low, to_high = grid_kernel(
        ana_edge_kernel,
        "ana_edges",
        (10**6, 4 * 10**6),
        in_specs=[pl.BlockSpec(memory_space=pltpu.HBM)],
        out_specs=[vmem] * 2,
        out_shape=[f32(snaps, ANA_ROWS, depth)] * 2,
        scratch_shapes=[scratch(snaps * comps, layers, 16, LANES)] * 2 + [pltpu.SemaphoreType.DMA((2 * snaps,))],
    )(pltpu.with_memory_space_constraint(tiles, pltpu.HBM))
    from_low, from_high = exchange(to_low, to_high, "ana")

    weight, pool = grid_kernel(
        functools.partial(weight_kernel, POOL_PARTS),
        "weights",
        (10**6, 10**6),
        in_specs=[vmem],
        out_specs=[vmem] * 2,
        out_shape=[f32(layers * columns, depth), jax.ShapeDtypeStruct((256 * POOL_PARTS, 256), jnp.bfloat16)],
        scratch_shapes=[scratch(2, layers * columns, LANES)],
    )(sample_index.reshape(samples // LANES, LANES))

    *fields, own_force, to_before, to_after = grid_kernel(
        load_kernel,
        "load",
        (10**8, 6 * 10**6),
        in_specs=[pl.BlockSpec(memory_space=pltpu.HBM), pl.BlockSpec(memory_space=pl.ANY)],
        out_specs=[vmem] * 6,
        out_shape=[f32(snaps, layers, columns, depth)] * 4 + [f32(snaps, BULK_ROWS, depth)] * 2,
        scratch_shapes=[pltpu.SemaphoreType.DMA((snaps * comps,))],
    )(pltpu.with_memory_space_constraint(source, pltpu.HBM), to_low)
    from_before, from_after = exchange(to_before, to_after, "brick")

    to_before, to_after = grid_kernel(
        fix_kernel,
        "fix",
        (10**5, 10**6),
        in_specs=[vmem] * 4,
        out_specs=[vmem] * 2,
        out_shape=[f32(snaps, FIX_ROWS, depth)] * 2,
    )(fields[1], own_force, from_low, from_high)
    before_fix, after_fix = exchange(to_before, to_after, "brick")

    split_shape = lambda count: pltpu.VMEM((3 * 32 * count, 256 * POOL_PARTS), jnp.bfloat16)
    force, press, outgoing = grid_kernel(
        functools.partial(inner_kernel, POOL_PARTS),
        "inner_layers",
        (4 * 10**9, 2 * 10**7),
        in_specs=[smem] + [vmem] * 8,
        out_specs=[vmem] * 3,
        out_shape=[f32(snaps, layers, columns, depth)] * 2 + [f32(bricks, comps, 32, LANES)],
        scratch_shapes=[
            scratch(4, layers, depth),
            split_shape(layers - 2 * MARGIN),
            scratch(2, 3 * 32 * (layers - 2 * MARGIN), LANES),
        ],
    )(owner_table, *fields, own_force, weight, pool, from_low, from_high)
    return grid_kernel(
        functools.partial(outer_kernel, POOL_PARTS),
        "outer_layers",
        (3 * 10**9, 10**7),
        in_specs=[smem] + [vmem] * 14,
        out_specs=vmem,
        out_shape=f32(bricks, comps, 32, LANES),
        scratch_shapes=[
            scratch(6, columns, depth),
            scratch(2 * MARGIN, columns, depth),
            scratch(2, 32, depth),
            scratch(2, layers, depth),
            split_shape(2 * MARGIN),
            scratch(2, 3 * 32 * 2 * MARGIN, LANES),
        ],
        input_output_aliases={14: 0},
    )(owner_table, *fields, weight, pool, from_low, from_high, from_before, from_after, before_fix, after_fix, force, press, outgoing)


def per_device(provisional, sample_index, owner_table, weighted_basis):
    snaps = provisional.shape[0]
    rank_count = weighted_basis.shape[0]
    devices = lax.axis_size("brick") * lax.axis_size("ana")
    total_rows = 3.0 * sample_index.shape[2] * devices
    outgoing = front(provisional, sample_index, owner_table)
    arrived = lax.all_to_all(outgoing, "brick", split_axis=0, concat_axis=0, tiled=True)
    basis = jnp.transpose(weighted_basis, (1, 0, 2))
    new_basis, core = tail(basis, arrived, WIDTH, total_rows, devices)
    count = rank_count + snaps
    return (jnp.transpose(new_basis, (1, 0, 2)), core[:count, :count])


def solution(mesh):
    placed = (
        P(None, None, "brick", "ana", None),
        P("brick", "ana", None),
        P(),
        P(None, None, ("brick", "ana")),
    )
    return jax.shard_map(
        per_device,
        mesh=mesh,
        in_specs=placed,
        out_specs=(P(None, None, ("brick", "ana")), P()),
        check_vma=False,
    )
```

```python
import functools
import jax
import jax.numpy as jnp
from jax import lax
from jax.experimental import pallas as pl
from jax.experimental.pallas import tpu as pltpu
from jax.sharding import PartitionSpec as P

LANES = 128
PACK = 24
GRAM = 20
POOL_PARTS = 2
WIDTH = 8192
SLOTS = 4
VMEM_LIMIT = 20 * 1024 * 1024


def split_pieces(block):
    high = block.astype(jnp.bfloat16)
    return high, (block - high.astype(jnp.float32)).astype(jnp.bfloat16)


def sample_pieces(arrived_ref, c, start, width):
    at = lax.broadcasted_iota(jnp.int32, (8, LANES), 0)
    tiles = []
    for b in range(start // 1024, (start + width) // 1024):
        for n in range(0, 32, 8):
            both = arrived_ref[b, c, n : n + 8, :]
            high = both.astype(jnp.bfloat16).astype(jnp.float32)
            low = both - high
            tiles.append(jnp.where(at < 4, high, pltpu.roll(low, 4, 0)))
            tiles.append(jnp.where(at < 4, pltpu.roll(high, 4, 0), low))
    rows = jnp.concatenate(tiles, axis=1)
    return jnp.concatenate([rows, rows], axis=0).astype(jnp.bfloat16)


def stacked_pieces(basis_ref, arrived_ref, c, start, width, order):
    large = split_pieces(basis_ref[c, :, start : start + width])
    return jnp.concatenate([large[p] for p in order] + [sample_pieces(arrived_ref, c, start, width)], axis=0)


def gram_kernel(width, scale, basis_ref, arrived_ref, out_ref):
    comps, rank_count, columns = basis_ref.shape
    total = 0.0
    for c in range(comps):
        for start in range(0, columns, width):
            pieces = stacked_pieces(basis_ref, arrived_ref, c, start, width, (0, 1))
            total = total + lax.dot_general(
                pieces, pieces, (((1,), (1,)), ((), ())), preferred_element_type=jnp.float32
            )
    total = jnp.concatenate([total, jnp.zeros((total.shape[0], LANES - total.shape[1]), jnp.float32)], axis=1)
    lane_at = lax.broadcasted_iota(jnp.int32, total.shape, 1)
    left = jnp.where(lane_at < 16, total, pltpu.roll(total, LANES - 20, 1)) + pltpu.roll(total, LANES - 16, 1)
    left = jnp.where(lane_at < GRAM, left, 0.0) * scale
    row_at = lax.broadcasted_iota(jnp.int32, (8, LANES), 0)
    small = jnp.where(row_at < 4, left[32:40] + pltpu.roll(left[32:40], 4, 0), 0.0)
    packed = left[0:8] + left[16:24]
    packed = packed + pltpu.roll(left[8:16] + left[24:32], GRAM, 1) + pltpu.roll(small, 2 * GRAM, 1)
    packed = packed[0:4] + pltpu.roll(packed, 3 * GRAM, 1)[4:8]
    out_ref[...] = jnp.broadcast_to(packed[None], out_ref.shape)


def factor(tiles, count, block):
    row_at = [lax.broadcasted_iota(jnp.int32, (8, LANES), 0) + 8 * t for t in range(3)]
    lane_at = lax.broadcasted_iota(jnp.int32, (8, LANES), 1)
    work = [jnp.where(lane_at < PACK, tiles[t], 0.0) + jnp.where(lane_at == row_at[t] + 32, 1.0, 0.0) for t in range(3)]
    diagonal = [jnp.ones((8, LANES), jnp.float32)] * 3

    def spread(piece):
        return jnp.broadcast_to(piece, (8, LANES))

    for j in range(0, count, block):
        later = [t for t in range(3) if j + block < count and 8 * t + 8 > j + block]
        rows = [spread(work[(j + q) // 8][(j + q) % 8 : (j + q) % 8 + 1]) for q in range(block)]
        cols = [{t: spread(work[t][:, j + q : j + q + 1]) for t in later} for q in range(block)]
        pivots = [[spread(rows[q][:, j + r : j + r + 1]) if r >= q else None for r in range(block)] for q in range(block)]
        for q in range(block):
            inverse = 1.0 / pivots[q][q]
            for r in range(q + 1, block):
                ratio = pivots[q][r] * inverse
                rows[r] = rows[r] - ratio * rows[q]
                for t in later:
                    cols[r][t] = cols[r][t] - ratio * cols[q][t]
                for u in range(r, block):
                    pivots[r][u] = pivots[r][u] - ratio * pivots[q][u]
            for t in later:
                ratio = jnp.where(row_at[t] >= j + block, cols[q][t] * inverse, 0.0)
                work[t] = work[t] - ratio * rows[q]
            t = (j + q) // 8
            work[t] = jnp.where(row_at[t] == j + q, rows[q], work[t])
            diagonal[t] = jnp.where(row_at[t] == j + q, pivots[q][q], diagonal[t])
    work = [work[t] / jnp.sqrt(diagonal[t]) for t in range(3)]
    upper = [jnp.where((lane_at >= row_at[t]) & (lane_at < PACK), work[t], 0.0) for t in range(3)]
    inverse = jnp.concatenate([pltpu.roll(work[t], LANES - 32, 1)[:, :PACK] for t in range(3)], axis=0)
    return upper, inverse


def apply_kernel(width, slots, basis_ref, arrived_ref, packed_ref, out_ref, core_ref, left_ref, slot_ref, sem):
    comps, rank_count, columns = basis_ref.shape
    count = out_ref.shape[1]
    packed = jnp.sum(packed_ref[...], axis=0)
    packed = jnp.concatenate([packed, pltpu.roll(packed, LANES - 3 * GRAM, 1)], axis=0)
    lane_at = lax.broadcasted_iota(jnp.int32, packed.shape, 1)
    tiles = [packed, pltpu.roll(packed, LANES - GRAM, 1), pltpu.roll(packed, LANES - 2 * GRAM, 1)]
    tiles = [jnp.where(lane_at < GRAM, tile, 0.0) for tile in tiles]
    upper, inverse = factor(tiles, count, count // 2)
    for t in range(3):
        core_ref[8 * t : 8 * t + 8, :] = upper[t]
    high, low = [piece.astype(jnp.float32) for piece in split_pieces(inverse)]
    order = (high, high, low)
    left = [piece[:, :rank_count] for piece in order] + [piece[:, rank_count:count] for piece in order]
    left.append(jnp.zeros((PACK, 16 - 4 * len(order)), jnp.float32))
    left_ref[...] = jnp.concatenate(left, axis=1).astype(jnp.bfloat16)

    blocks = [(c, start) for c in range(comps) for start in range(0, columns, width)]
    copies = []
    for n, (c, start) in enumerate(blocks):
        if n >= slots:
            copies[n - slots].wait()
        pieces = stacked_pieces(basis_ref, arrived_ref, c, start, width, (0, 1, 0))
        product = jnp.dot(left_ref[...], pieces, preferred_element_type=jnp.float32)
        slot = n % slots
        slot_ref[slot] = product[:count]
        copy = pltpu.make_async_copy(slot_ref.at[slot], out_ref.at[c, :, start : start + width], sem.at[slot])
        copy.start()
        copies.append(copy)
    for copy in copies[-slots:]:
        copy.wait()


def tail(basis, arrived, width, total_rows, devices):
    comps, rank_count, rows = basis.shape
    vmem = pl.BlockSpec(memory_space=pltpu.VMEM)
    copies = grid_kernel(
        functools.partial(gram_kernel, width, 1.0 / total_rows),
        "gram",
        (10**9, 10**7),
        in_specs=[vmem, vmem],
        out_specs=vmem,
        out_shape=jax.ShapeDtypeStruct((devices, 4, LANES), jnp.float32),
    )(basis, arrived)
    partial_sums = lax.all_to_all(copies, ("brick", "ana"), 0, 0, tiled=True)
    count = rank_count + 4
    return grid_kernel(
        functools.partial(apply_kernel, width, SLOTS),
        "apply",
        (10**9, 2 * 10**7),
        in_specs=[vmem] * 3,
        out_specs=[pl.BlockSpec(memory_space=pltpu.HBM), vmem],
        out_shape=[
            jax.ShapeDtypeStruct((comps, count, rows), jnp.float32),
            jax.ShapeDtypeStruct((PACK, LANES), jnp.float32),
        ],
        scratch_shapes=[
            pltpu.VMEM((PACK, rank_count * 3 + 16), jnp.bfloat16),
            pltpu.VMEM((SLOTS, count, width), jnp.float32),
            pltpu.SemaphoreType.DMA((SLOTS,)),
        ],
    )(basis, arrived, partial_sums)


ANA_ROWS = 56
BULK_ROWS = 96
FIX_ROWS = 16
MARGIN = 3
PADDED = 48


def depth_pair(field):
    lanes = field.shape[-1]
    lane_at = lax.broadcasted_iota(jnp.int32, field.shape, field.ndim - 1)
    after = jnp.where(lane_at == lanes - 1, 0.0, pltpu.roll(field, lanes - 1, field.ndim - 1))
    before = jnp.where(lane_at == 0, 0.0, pltpu.roll(field, 1, field.ndim - 1))
    return after, before


def row_pair(field, after_row, before_row):
    rows = field.shape[0]
    row_at = lax.broadcasted_iota(jnp.int32, field.shape, 0)
    after = jnp.where(row_at == rows - 1, after_row, pltpu.roll(field, rows - 1, 0))
    before = jnp.where(row_at == 0, before_row, pltpu.roll(field, 1, 0))
    return after, before


def inside(axis):
    at = lax.axis_index(axis)
    return at > 0, at < lax.axis_size(axis) - 1


def difference(pair):
    return pair[0] - pair[1]


def halves(row):
    return [row[:, LANES * h : LANES * h + LANES] for h in range(2)]


def put_rows(ref, at, start, rows):
    for h, half in enumerate(halves(rows)):
        ref[(*at, h, slice(8 + start, 8 + start + rows.shape[0]), slice(None))] = half


def get_rows(ref, at, start, size):
    return jnp.concatenate([ref[(*at, h, slice(8 + start, 8 + start + size), slice(None))] for h in range(2)], axis=1)


def relaxed(field, around):
    return (field + around * (1.0 / 6.0)) * (1.0 / 6.0)


def ana_edge_kernel(tiles_ref, to_low_ref, to_high_ref, low_ref, high_ref, sem):
    snaps = to_low_ref.shape[0]
    fields, layers, rows, lanes = low_ref.shape
    last = tiles_ref.shape[2] - 1
    copies = []
    for s in range(snaps):
        span = pl.ds(3 * s, 3)
        for n, (at, ref) in enumerate(((0, low_ref), (last, high_ref))):
            copies.append(pltpu.make_async_copy(tiles_ref.at[span, :, at], ref.at[span], sem.at[2 * s + n]))
    for copy in copies:
        copy.start()
    flat = (fields * layers * rows, lanes)

    def column(ref, s, c, j):
        start = (s * 3 + c) * layers * rows + j
        return jnp.concatenate(
            [ref[pl.ds(start + 8 * half, layers, stride=rows), :] for half in range(2)], axis=1
        )

    zero_row = jnp.zeros((1, 2 * lanes), jnp.float32)
    for s in range(snaps):
        for n, (side_ref, out_ref, edge, second, third, sign) in enumerate(
            ((low_ref, to_low_ref, 0, 1, 2, 1.0), (high_ref, to_high_ref, 7, 6, 5, -1.0))
        ):
            copies[2 * s + n].wait()
            ref = side_ref.reshape(*flat)
            speed = [column(ref, s, 0, j) for j in (edge, second)]
            cross = [column(ref, s, 1, j) for j in (edge, second, third)]
            deep = [column(ref, s, 2, j) for j in (edge, second)]
            beside = (sign * cross[1], sign * (cross[2] - cross[0]))
            out_ref[s, 0:16, :] = cross[0]
            for n in range(2):
                along = difference(row_pair(speed[n], zero_row, zero_row))
                out_ref[s, 16 + 16 * n : 32 + 16 * n, :] = -0.5 * (
                    along + beside[n] + difference(depth_pair(deep[n]))
                )
            out_ref[s, 48:56, :] = jnp.concatenate(
                [speed[0][0:1], speed[1][0:1], speed[0][15:16], speed[1][15:16]] + [zero_row] * 4,
                axis=0,
            )


def load_kernel(source_ref, _, along_ref, cross_ref, deep_ref, force_ref, to_low_ref, to_high_ref, sem):
    snaps, layers = force_ref.shape[:2]
    fields = (along_ref, cross_ref, deep_ref)
    copies = [
        pltpu.make_async_copy(source_ref.at[n], fields[n % 3].at[n // 3], sem.at[n]) for n in range(3 * snaps)
    ]
    for copy in copies:
        copy.start()
    for s in range(snaps):
        for copy in copies[3 * s : 3 * s + 3]:
            copy.wait()
        for i in range(layers):
            along = 0.0
            if i < layers - 1:
                along = along + along_ref[s, i + 1]
            if i > 0:
                along = along - along_ref[s, i - 1]
            cross = row_pair(cross_ref[s, i], 0.0, 0.0)
            force_ref[s, i] = -0.5 * (
                along + difference(cross) + difference(depth_pair(deep_ref[s, i]))
            )
        for out_ref, layer, second in ((to_low_ref, 0, 1), (to_high_ref, layers - 1, layers - 2)):
            out_ref[s, 0:32, :] = force_ref[s, second]
            out_ref[s, 32:64, :] = force_ref[s, layer]
            out_ref[s, 64:96, :] = along_ref[s, layer]


def fix_kernel(cross_ref, force_ref, from_low_ref, from_high_ref, to_low_ref, to_high_ref):
    layers = force_ref.shape[1]
    keep_low, keep_high = inside("ana")
    for s in range(to_low_ref.shape[0]):
        for out_ref, layer, second, pillar in ((to_low_ref, 0, 1, 48), (to_high_ref, layers - 1, layers - 2, 50)):

            def halo(side_ref, keep, row):
                return jnp.where(keep, side_ref[s, row : row + 1, :], 0.0)

            cross = cross_ref[s, layer]
            row = 16 + layer
            below = jnp.where(keep_low, from_low_ref[s, row : row + 1, :] - 0.5 * cross[0:1], 0.0)
            above = jnp.where(keep_high, from_high_ref[s, row : row + 1, :] + 0.5 * cross[31:32], 0.0)
            rows = [
                force_ref[s, layer, 0:1, :] + 0.5 * halo(from_low_ref, keep_low, layer),
                force_ref[s, layer, 31:32, :] - 0.5 * halo(from_high_ref, keep_high, layer),
                force_ref[s, second, 0:1, :] + 0.5 * halo(from_low_ref, keep_low, second),
                force_ref[s, second, 31:32, :] - 0.5 * halo(from_high_ref, keep_high, second),
                halo(from_low_ref, keep_low, pillar + 1),
                halo(from_low_ref, keep_low, pillar),
                halo(from_high_ref, keep_high, pillar),
                halo(from_high_ref, keep_high, pillar + 1),
                below,
                above,
            ]
            rows = rows + [jnp.zeros_like(below)] * (FIX_ROWS - len(rows))
            out_ref[s] = jnp.concatenate(rows, axis=0)


def sample_layers(s, parts, layers, fields, owner, weight_ref, pool_ref, out_ref, split_ref, pooled_ref, press):
    count = len(layers)
    for n, i in enumerate(layers):
        centre = get_rows(*press(i), 0, 32)
        gradient = (
            get_rows(*press(i + 1), 0, 32) - get_rows(*press(i - 1), 0, 32),
            get_rows(*press(i), 1, 32) - get_rows(*press(i), -1, 32),
            difference(depth_pair(centre)),
        )
        weight = weight_ref[32 * i : 32 * i + 32, :]
        for c in range(3):
            kept = (fields[c][s, i] - 0.5 * gradient[c]) * weight
            row = 32 * (c * count + n)
            for p in range(parts):
                piece = kept.astype(jnp.bfloat16)
                split_ref[row : row + 32, 256 * p : 256 * p + 256] = piece
                if p < parts - 1:
                    kept = kept - piece.astype(jnp.float32)
    pooled = jnp.dot(split_ref[...], pool_ref[...], preferred_element_type=jnp.float32)
    pooled_ref[0] = pooled[:, :LANES]
    pooled_ref[1] = pooled[:, LANES:]
    rows = 3 * count * 32
    flat = pooled_ref.reshape(2 * rows, LANES)
    for n, i in enumerate(layers):
        for half in range(2):
            place = owner(2 * i + half)
            for c in range(3):
                start = 32 * (c * count + n) + 16 * half
                tile = flat[pl.ds(start, 8, stride=2), :] + flat[pl.ds(start + rows + 1, 8, stride=2), :]
                out_ref[place, c, pl.ds(s, 8, stride=4), :] = tile


def inner_kernel(
    parts, owner_ref, along_ref, cross_ref, deep_ref, own_force_ref, weight_ref, pool_ref, low_ref, high_ref,
    force_ref, press_ref, out_ref, sides_ref, split_ref, pooled_ref,
):
    layers = along_ref.shape[1]
    keep_low, keep_high = inside("ana")
    brick = lax.axis_index("brick")

    def snapshot(s):
        side_ref = sides_ref.at[s]
        def halo(ref, keep, start, size=1):
            return jnp.where(keep, ref[s, start : start + size, :], 0.0)

        row_at = lax.broadcasted_iota(jnp.int32, (8, along_ref.shape[3]), 0)
        for i in range(layers):
            first, last = own_force_ref[s, i, 0:8, :], own_force_ref[s, i, 24:32, :]
            put_rows(force_ref, (s, i), 0, jnp.where(row_at == 0, first + 0.5 * halo(low_ref, keep_low, i), first))
            put_rows(force_ref, (s, i), 8, own_force_ref[s, i, 8:24, :])
            put_rows(force_ref, (s, i), 24, jnp.where(row_at == 7, last - 0.5 * halo(high_ref, keep_high, i), last))

        for side, ref, keep, row, sign in ((0, low_ref, keep_low, 0, -0.5), (1, high_ref, keep_high, 31, 0.5)):
            own_cross = jnp.concatenate([cross_ref[s, i, row : row + 1, :] for i in range(layers)], axis=0)
            own_force = jnp.concatenate([get_rows(force_ref, (s, i), row, 1) for i in range(layers)], axis=0)
            edge = ref[s, 16:32, :] + sign * own_cross
            zero_row = jnp.zeros((1, edge.shape[1]), jnp.float32)
            around = sum(row_pair(edge, zero_row, zero_row)) + ref[s, 32:48, :] + own_force
            around = around + sum(depth_pair(edge))
            side_ref[2 + side] = jnp.where(keep, edge, 0.0)
            side_ref[side] = jnp.where(keep, relaxed(edge, around), 0.0)

        for i in range(layers):
            put_rows(force_ref, (s, i), -1, side_ref[2, i : i + 1, :])
            put_rows(force_ref, (s, i), 32, side_ref[3, i : i + 1, :])
        for i in range(MARGIN - 1, layers - MARGIN + 1):
            field = get_rows(force_ref, (s, i), 0, 32)
            around = get_rows(force_ref, (s, i + 1), 0, 32) + get_rows(force_ref, (s, i - 1), 0, 32)
            around = around + (get_rows(force_ref, (s, i), 1, 32) + get_rows(force_ref, (s, i), -1, 32))
            put_rows(press_ref, (s, i), 0, relaxed(field, around + sum(depth_pair(field))))
            put_rows(press_ref, (s, i), -1, side_ref[0, i : i + 1, :])
            put_rows(press_ref, (s, i), 32, side_ref[1, i : i + 1, :])

        sample_layers(
            s, parts, list(range(MARGIN, layers - MARGIN)), (along_ref, cross_ref, deep_ref),
            lambda k: owner_ref[brick, k], weight_ref, pool_ref,
            out_ref, split_ref.at[s], pooled_ref.at[s],
            lambda i: (press_ref, (s, i)),
        )
    for s in range(along_ref.shape[0]):
        snapshot(s)


def outer_kernel(
    parts, owner_ref, along_ref, cross_ref, deep_ref, weight_ref, pool_ref, low_ref, high_ref, before_ref, after_ref,
    before_fix_ref, after_fix_ref, inner_force_ref, inner_press_ref, _, out_ref, forces_ref, presses_ref, side_forces_ref, side_presses_ref,
    split_ref, pooled_ref,
):
    layers = along_ref.shape[1]
    keep_before, keep_after = inside("brick")
    keep_low, keep_high = inside("ana")
    brick = lax.axis_index("brick")

    def snapshot(s):
        force_ref, press_ref = forces_ref.at[s], presses_ref.at[s]
        side_force_ref, side_press_ref = side_forces_ref.at[s], side_presses_ref.at[s]
        def halo(ref, keep, start, size=1):
            return jnp.where(keep, ref[s, start : start + size, :], 0.0)

        def fixed(ref, fix_ref, start, row):
            field = ref[s, start : start + 32, :]
            row_at = lax.broadcasted_iota(jnp.int32, field.shape, 0)
            field = jnp.where(row_at == 0, fix_ref[s, row : row + 1, :], field)
            return jnp.where(row_at == 31, fix_ref[s, row + 1 : row + 2, :], field)

        first, last = along_ref[s, 0], along_ref[s, layers - 1]
        edges = (
            jnp.where(keep_before, fixed(before_ref, before_fix_ref, 0, 2), 0.0),
            jnp.where(keep_before, fixed(before_ref, before_fix_ref, 32, 0) - 0.5 * first, 0.0),
            get_rows(inner_force_ref, (s, 0), 0, 32) + 0.5 * halo(before_ref, keep_before, 64, 32),
            get_rows(inner_force_ref, (s, layers - 1), 0, 32) - 0.5 * halo(after_ref, keep_after, 64, 32),
            jnp.where(keep_after, fixed(after_ref, after_fix_ref, 32, 0) + 0.5 * last, 0.0),
            jnp.where(keep_after, fixed(after_ref, after_fix_ref, 0, 2), 0.0),
        )
        for n, edge in enumerate(edges):
            put_rows(force_ref, (n,), 0, edge)

        def force(i):
            if i < 1:
                return force_ref, (i + 2,)
            if i > layers - 2:
                return force_ref, (i - layers + 4,)
            return inner_force_ref, (s, i)

        for side, ref, keep, far, near, corner, row, sign in (
            (0, low_ref, keep_low, 4, 5, 8, 0, -0.5),
            (1, high_ref, keep_high, 7, 6, 9, 31, 0.5),
        ):
            own_cross = jnp.concatenate([cross_ref[s, i, row : row + 1, :] for i in range(layers)], axis=0)
            own_force = jnp.concatenate(
                [get_rows(*force(i), row, 1) for i in range(layers)],
                axis=0,
            )
            row_at = lax.broadcasted_iota(jnp.int32, own_force.shape, 0)

            def ends(at):
                first = 0.5 * halo(before_fix_ref, keep_before, at)
                last = -0.5 * halo(after_fix_ref, keep_after, at)
                return jnp.where(row_at == 0, first, 0.0) + jnp.where(row_at == layers - 1, last, 0.0)

            edge = jnp.where(keep, ref[s, 16:32, :] + sign * own_cross + ends(near), 0.0)
            beyond = jnp.where(keep, ref[s, 32:48, :] + ends(far), 0.0)
            corner_before = jnp.where(keep_before, halo(before_fix_ref, keep, corner) - 0.5 * halo(ref, keep, 48), 0.0)
            corner_after = jnp.where(keep_after, halo(after_fix_ref, keep, corner) + 0.5 * halo(ref, keep, 50), 0.0)
            around = sum(row_pair(edge, corner_after, corner_before)) + beyond + own_force
            around = around + sum(depth_pair(edge))
            side_press_ref[side] = jnp.where(keep, relaxed(edge, around), 0.0)
            side_force_ref[side, 8:24, :] = edge
            side_force_ref[side, 7:8, :] = corner_before
            side_force_ref[side, 24:25, :] = corner_after

        low_layers, high_layers = list(range(-1, MARGIN - 1)), list(range(layers - MARGIN + 1, layers + 1))
        place = {i: n for n, i in enumerate(low_layers + high_layers)}
        for i in (-1, 0, layers - 1, layers):
            put_rows(*force(i), -1, side_force_ref[0, 8 + i : 9 + i, :])
            put_rows(*force(i), 32, side_force_ref[1, 8 + i : 9 + i, :])
        for i in place:
            field = get_rows(*force(i), 0, 32)
            around = get_rows(*force(i + 1), 0, 32) + get_rows(*force(i - 1), 0, 32)
            around = around + (get_rows(*force(i), 1, 32) + get_rows(*force(i), -1, 32))
            press = relaxed(field, around + sum(depth_pair(field)))
            if i == -1:
                press = jnp.where(keep_before, press, 0.0)
            if i == layers:
                press = jnp.where(keep_after, press, 0.0)
            put_rows(press_ref, (place[i],), 0, press)
            if 0 <= i < layers:
                put_rows(press_ref, (place[i],), -1, side_press_ref[0, i : i + 1, :])
                put_rows(press_ref, (place[i],), 32, side_press_ref[1, i : i + 1, :])

        sample_layers(
            s, parts, list(range(MARGIN)) + list(range(layers - MARGIN, layers)), (along_ref, cross_ref, deep_ref),
            lambda k: owner_ref[brick, k], weight_ref, pool_ref, out_ref, split_ref.at[s], pooled_ref.at[s],
            lambda i: (press_ref, (place[i],)) if i in place else (inner_press_ref, (s, i)),
        )
    for s in range(along_ref.shape[0]):
        snapshot(s)


def weight_kernel(parts, index_ref, out_ref, pool_ref, wide_ref):
    pool_ref[...] = pooling(parts)
    rows = index_ref.shape[0]
    at = lax.broadcasted_iota(jnp.int32, (rows, LANES), 0) * LANES + lax.broadcasted_iota(jnp.int32, (rows, LANES), 1)
    offset = (index_ref[...] - 4 * at).astype(jnp.float32).astype(jnp.bfloat16)
    source = lax.broadcasted_iota(jnp.int32, (LANES, 512), 0)
    target = lax.broadcasted_iota(jnp.int32, (LANES, 512), 1)
    expand = jnp.where(target // 4 == source, 1.0, 0.0).astype(jnp.bfloat16)
    wide = jnp.dot(offset, expand, preferred_element_type=jnp.float32)
    lane_at = lax.broadcasted_iota(jnp.int32, wide.shape, 1)
    hit = jnp.where(wide == (lane_at % 4).astype(jnp.float32), 1.0, 0.0)
    for half in range(2):
        for kt in range(2):
            wide_ref[kt, pl.ds(half, rows, stride=2), :] = hit[:, 256 * half + 128 * kt : 256 * half + 128 * kt + 128]
    for kt in range(2):
        out_ref[:, 128 * kt : 128 * kt + 128] = wide_ref[kt]


def pooling(parts):
    source = lax.broadcasted_iota(jnp.int32, (256 * parts, 256), 0) % 256
    target = lax.broadcasted_iota(jnp.int32, (256 * parts, 256), 1)
    low = (target < 64) & (source // 4 == target)
    high = (target >= 192) & (source // 4 == target - 192)
    return jnp.where(low | high, 1.0, 0.0).astype(jnp.bfloat16)


def exchange(to_before, to_after, axis):
    devices = lax.axis_size(axis)
    up = [(i, (i + 1) % devices) for i in range(devices)]
    down = [(j, i) for i, j in up]
    return lax.ppermute(to_after, axis, up), lax.ppermute(to_before, axis, down)


def grid_kernel(kernel, name, cost, **kwargs):
    flops, data = cost
    return pl.pallas_call(
        kernel,
        compiler_params=pltpu.CompilerParams(vmem_limit_bytes=VMEM_LIMIT),
        cost_estimate=pl.CostEstimate(flops=flops, bytes_accessed=data, transcendentals=0),
        name=name,
        **kwargs,
    )


def front(provisional, sample_index, owner_table):
    snaps, comps, layers, columns, depth = provisional.shape
    bricks = lax.axis_size("brick")
    smem = pl.BlockSpec(memory_space=pltpu.SMEM)
    vmem = pl.BlockSpec(memory_space=pltpu.VMEM)
    samples = layers * columns * depth // 4
    source = provisional.reshape(snaps * comps, layers, columns, depth)
    f32 = lambda *shape: jax.ShapeDtypeStruct(shape, jnp.float32)
    scratch = lambda *shape: pltpu.VMEM(shape, jnp.float32)

    tiles = source.reshape(snaps * comps, layers, columns // 8, 8, 2, LANES)
    tiles = tiles.transpose(0, 1, 2, 4, 3, 5).reshape(snaps * comps, layers, columns // 8, 16, LANES)
    to_low, to_high = grid_kernel(
        ana_edge_kernel,
        "ana_edges",
        (10**6, 4 * 10**6),
        in_specs=[pl.BlockSpec(memory_space=pltpu.HBM)],
        out_specs=[vmem] * 2,
        out_shape=[f32(snaps, ANA_ROWS, depth)] * 2,
        scratch_shapes=[scratch(snaps * comps, layers, 16, LANES)] * 2 + [pltpu.SemaphoreType.DMA((2 * snaps,))],
    )(pltpu.with_memory_space_constraint(tiles, pltpu.HBM))
    from_low, from_high = exchange(to_low, to_high, "ana")

    weight, pool = grid_kernel(
        functools.partial(weight_kernel, POOL_PARTS),
        "weights",
        (10**6, 10**6),
        in_specs=[vmem],
        out_specs=[vmem] * 2,
        out_shape=[f32(layers * columns, depth), jax.ShapeDtypeStruct((256 * POOL_PARTS, 256), jnp.bfloat16)],
        scratch_shapes=[scratch(2, layers * columns, LANES)],
    )(sample_index.reshape(samples // LANES, LANES))

    *fields, own_force, to_before, to_after = grid_kernel(
        load_kernel,
        "load",
        (10**8, 6 * 10**6),
        in_specs=[pl.BlockSpec(memory_space=pltpu.HBM), pl.BlockSpec(memory_space=pl.ANY)],
        out_specs=[vmem] * 6,
        out_shape=[f32(snaps, layers, columns, depth)] * 4 + [f32(snaps, BULK_ROWS, depth)] * 2,
        scratch_shapes=[pltpu.SemaphoreType.DMA((snaps * comps,))],
    )(pltpu.with_memory_space_constraint(source, pltpu.HBM), to_low)
    from_before, from_after = exchange(to_before, to_after, "brick")

    to_before, to_after = grid_kernel(
        fix_kernel,
        "fix",
        (10**5, 10**6),
        in_specs=[vmem] * 4,
        out_specs=[vmem] * 2,
        out_shape=[f32(snaps, FIX_ROWS, depth)] * 2,
    )(fields[1], own_force, from_low, from_high)
    before_fix, after_fix = exchange(to_before, to_after, "brick")

    split_shape = lambda count: pltpu.VMEM((snaps, 3 * 32 * count, 256 * POOL_PARTS), jnp.bfloat16)
    force, press, outgoing = grid_kernel(
        functools.partial(inner_kernel, POOL_PARTS),
        "inner_layers",
        (4 * 10**9, 2 * 10**7),
        in_specs=[smem] + [vmem] * 8,
        out_specs=[vmem] * 3,
        out_shape=[f32(snaps, layers, 2, PADDED, LANES)] * 2 + [f32(bricks, comps, 32, LANES)],
        scratch_shapes=[
            scratch(snaps, 4, layers, depth),
            split_shape(layers - 2 * MARGIN),
            scratch(snaps, 2, 3 * 32 * (layers - 2 * MARGIN), LANES),
        ],
    )(owner_table, *fields, own_force, weight, pool, from_low, from_high)
    return grid_kernel(
        functools.partial(outer_kernel, POOL_PARTS),
        "outer_layers",
        (3 * 10**9, 10**7),
        in_specs=[smem] + [vmem] * 14,
        out_specs=vmem,
        out_shape=f32(bricks, comps, 32, LANES),
        scratch_shapes=[
            scratch(snaps, 6, 2, PADDED, LANES),
            scratch(snaps, 2 * MARGIN, 2, PADDED, LANES),
            scratch(snaps, 2, 32, depth),
            scratch(snaps, 2, layers, depth),
            split_shape(2 * MARGIN),
            scratch(snaps, 2, 3 * 32 * 2 * MARGIN, LANES),
        ],
        input_output_aliases={14: 0},
    )(owner_table, *fields, weight, pool, from_low, from_high, from_before, from_after, before_fix, after_fix, force, press, outgoing)


def per_device(provisional, sample_index, owner_table, weighted_basis):
    snaps = provisional.shape[0]
    rank_count = weighted_basis.shape[0]
    devices = lax.axis_size("brick") * lax.axis_size("ana")
    total_rows = 3.0 * sample_index.shape[2] * devices
    outgoing = front(provisional, sample_index, owner_table)
    arrived = lax.all_to_all(outgoing, "brick", split_axis=0, concat_axis=0, tiled=True)
    basis = jnp.transpose(weighted_basis, (1, 0, 2))
    new_basis, core = tail(basis, arrived, WIDTH, total_rows, devices)
    count = rank_count + snaps
    return (jnp.transpose(new_basis, (1, 0, 2)), core[:count, :count])


def solution(mesh):
    placed = (
        P(None, None, "brick", "ana", None),
        P("brick", "ana", None),
        P(),
        P(None, None, ("brick", "ana")),
    )
    return jax.shard_map(
        per_device,
        mesh=mesh,
        in_specs=placed,
        out_specs=(P(None, None, ("brick", "ana")), P()),
        check_vma=False,
    )
```

```python
import functools
import jax
import jax.numpy as jnp
from jax import lax
from jax.experimental import pallas as pl
from jax.experimental.pallas import tpu as pltpu
from jax.sharding import PartitionSpec as P

LANES = 128
PACK = 24
GRAM = 20
POOL_PARTS = 2
WIDTH = 8192
SLOTS = 4
VMEM_LIMIT = 20 * 1024 * 1024


def split_pieces(block):
    high = block.astype(jnp.bfloat16)
    return high, (block - high.astype(jnp.float32)).astype(jnp.bfloat16)


def sample_pieces(arrived_ref, c, start, width):
    at = lax.broadcasted_iota(jnp.int32, (8, LANES), 0)
    tiles = []
    for b in range(start // 1024, (start + width) // 1024):
        for n in range(0, 32, 8):
            both = arrived_ref[b, c, n : n + 8, :]
            high = both.astype(jnp.bfloat16).astype(jnp.float32)
            low = both - high
            tiles.append(jnp.where(at < 4, high, pltpu.roll(low, 4, 0)))
            tiles.append(jnp.where(at < 4, pltpu.roll(high, 4, 0), low))
    rows = jnp.concatenate(tiles, axis=1)
    return jnp.concatenate([rows, rows], axis=0).astype(jnp.bfloat16)


def stacked_pieces(basis_ref, arrived_ref, c, start, width, order):
    large = split_pieces(basis_ref[c, :, start : start + width])
    return jnp.concatenate([large[p] for p in order] + [sample_pieces(arrived_ref, c, start, width)], axis=0)


def gram_kernel(width, scale, basis_ref, arrived_ref, out_ref):
    comps, rank_count, columns = basis_ref.shape
    total = 0.0
    for c in range(comps):
        for start in range(0, columns, width):
            pieces = stacked_pieces(basis_ref, arrived_ref, c, start, width, (0, 1))
            total = total + lax.dot_general(
                pieces, pieces, (((1,), (1,)), ((), ())), preferred_element_type=jnp.float32
            )
    total = jnp.concatenate([total, jnp.zeros((total.shape[0], LANES - total.shape[1]), jnp.float32)], axis=1)
    lane_at = lax.broadcasted_iota(jnp.int32, total.shape, 1)
    left = jnp.where(lane_at < 16, total, pltpu.roll(total, LANES - 20, 1)) + pltpu.roll(total, LANES - 16, 1)
    left = jnp.where(lane_at < GRAM, left, 0.0) * scale
    row_at = lax.broadcasted_iota(jnp.int32, (8, LANES), 0)
    small = jnp.where(row_at < 4, left[32:40] + pltpu.roll(left[32:40], 4, 0), 0.0)
    packed = left[0:8] + left[16:24]
    packed = packed + pltpu.roll(left[8:16] + left[24:32], GRAM, 1) + pltpu.roll(small, 2 * GRAM, 1)
    packed = packed[0:4] + pltpu.roll(packed, 3 * GRAM, 1)[4:8]
    out_ref[...] = jnp.broadcast_to(packed[None], out_ref.shape)


def factor(tiles, count, block):
    row_at = [lax.broadcasted_iota(jnp.int32, (8, LANES), 0) + 8 * t for t in range(3)]
    lane_at = lax.broadcasted_iota(jnp.int32, (8, LANES), 1)
    work = [jnp.where(lane_at < PACK, tiles[t], 0.0) + jnp.where(lane_at == row_at[t] + 32, 1.0, 0.0) for t in range(3)]
    diagonal = [jnp.ones((8, LANES), jnp.float32)] * 3

    def spread(piece):
        return jnp.broadcast_to(piece, (8, LANES))

    for j in range(0, count, block):
        later = [t for t in range(3) if j + block < count and 8 * t + 8 > j + block]
        rows = [spread(work[(j + q) // 8][(j + q) % 8 : (j + q) % 8 + 1]) for q in range(block)]
        cols = [{t: spread(work[t][:, j + q : j + q + 1]) for t in later} for q in range(block)]
        pivots = [[spread(rows[q][:, j + r : j + r + 1]) if r >= q else None for r in range(block)] for q in range(block)]
        for q in range(block):
            inverse = 1.0 / pivots[q][q]
            for r in range(q + 1, block):
                ratio = pivots[q][r] * inverse
                rows[r] = rows[r] - ratio * rows[q]
                for t in later:
                    cols[r][t] = cols[r][t] - ratio * cols[q][t]
                for u in range(r, block):
                    pivots[r][u] = pivots[r][u] - ratio * pivots[q][u]
            for t in later:
                ratio = jnp.where(row_at[t] >= j + block, cols[q][t] * inverse, 0.0)
                work[t] = work[t] - ratio * rows[q]
            t = (j + q) // 8
            work[t] = jnp.where(row_at[t] == j + q, rows[q], work[t])
            diagonal[t] = jnp.where(row_at[t] == j + q, pivots[q][q], diagonal[t])
    work = [work[t] / jnp.sqrt(diagonal[t]) for t in range(3)]
    upper = [jnp.where((lane_at >= row_at[t]) & (lane_at < PACK), work[t], 0.0) for t in range(3)]
    inverse = jnp.concatenate([pltpu.roll(work[t], LANES - 32, 1)[:, :PACK] for t in range(3)], axis=0)
    return upper, inverse


def apply_kernel(width, slots, basis_ref, arrived_ref, packed_ref, out_ref, core_ref, left_ref, slot_ref, sem):
    comps, rank_count, columns = basis_ref.shape
    count = out_ref.shape[1]
    packed = jnp.sum(packed_ref[...], axis=0)
    packed = jnp.concatenate([packed, pltpu.roll(packed, LANES - 3 * GRAM, 1)], axis=0)
    lane_at = lax.broadcasted_iota(jnp.int32, packed.shape, 1)
    tiles = [packed, pltpu.roll(packed, LANES - GRAM, 1), pltpu.roll(packed, LANES - 2 * GRAM, 1)]
    tiles = [jnp.where(lane_at < GRAM, tile, 0.0) for tile in tiles]
    upper, inverse = factor(tiles, count, count // 2)
    for t in range(3):
        core_ref[8 * t : 8 * t + 8, :] = upper[t]
    high, low = [piece.astype(jnp.float32) for piece in split_pieces(inverse)]
    order = (high, high, low)
    left = [piece[:, :rank_count] for piece in order] + [piece[:, rank_count:count] for piece in order]
    left.append(jnp.zeros((PACK, 16 - 4 * len(order)), jnp.float32))
    left_ref[...] = jnp.concatenate(left, axis=1).astype(jnp.bfloat16)

    blocks = [(c, start, width) for c in range(comps) for start in range(0, columns, width)]
    c, start, size = blocks[-1]
    blocks = [(0, 0, 2048), (0, 2048, width - 2048)] + blocks[1:-1]
    blocks = blocks + [(c, start, size - 2048), (c, start + size - 2048, 2048)]
    copies = []
    for n, (c, start, size) in enumerate(blocks):
        if n >= slots:
            copies[n - slots].wait()
        pieces = stacked_pieces(basis_ref, arrived_ref, c, start, size, (0, 1, 0))
        product = jnp.dot(left_ref[...], pieces, preferred_element_type=jnp.float32)
        slot = n % slots
        slot_ref[slot, :, 0:size] = product[:count]
        copy = pltpu.make_async_copy(
            slot_ref.at[slot, :, pl.ds(0, size)], out_ref.at[c, :, pl.ds(start, size)], sem.at[slot]
        )
        copy.start()
        copies.append(copy)
    for copy in copies[-slots:]:
        copy.wait()


def tail(basis, arrived, width, total_rows, devices):
    comps, rank_count, rows = basis.shape
    vmem = pl.BlockSpec(memory_space=pltpu.VMEM)
    copies = grid_kernel(
        functools.partial(gram_kernel, width, 1.0 / total_rows),
        "gram",
        (10**9, 10**7),
        in_specs=[vmem, vmem],
        out_specs=vmem,
        out_shape=jax.ShapeDtypeStruct((devices, 4, LANES), jnp.float32),
    )(basis, arrived)
    partial_sums = lax.all_to_all(copies, ("brick", "ana"), 0, 0, tiled=True)
    count = rank_count + 4
    return grid_kernel(
        functools.partial(apply_kernel, width, SLOTS),
        "apply",
        (10**9, 2 * 10**7),
        in_specs=[vmem] * 3,
        out_specs=[pl.BlockSpec(memory_space=pltpu.HBM), vmem],
        out_shape=[
            jax.ShapeDtypeStruct((comps, count, rows), jnp.float32),
            jax.ShapeDtypeStruct((PACK, LANES), jnp.float32),
        ],
        scratch_shapes=[
            pltpu.VMEM((PACK, rank_count * 3 + 16), jnp.bfloat16),
            pltpu.VMEM((SLOTS, count, width), jnp.float32),
            pltpu.SemaphoreType.DMA((SLOTS,)),
        ],
    )(basis, arrived, partial_sums)


ANA_ROWS = 56
BULK_ROWS = 96
FIX_ROWS = 16
MARGIN = 3
PADDED = 48


def depth_pair(field):
    lanes = field.shape[-1]
    lane_at = lax.broadcasted_iota(jnp.int32, field.shape, field.ndim - 1)
    after = jnp.where(lane_at == lanes - 1, 0.0, pltpu.roll(field, lanes - 1, field.ndim - 1))
    before = jnp.where(lane_at == 0, 0.0, pltpu.roll(field, 1, field.ndim - 1))
    return after, before


def row_pair(field, after_row, before_row):
    rows = field.shape[0]
    row_at = lax.broadcasted_iota(jnp.int32, field.shape, 0)
    after = jnp.where(row_at == rows - 1, after_row, pltpu.roll(field, rows - 1, 0))
    before = jnp.where(row_at == 0, before_row, pltpu.roll(field, 1, 0))
    return after, before


def inside(axis):
    at = lax.axis_index(axis)
    return at > 0, at < lax.axis_size(axis) - 1


def difference(pair):
    return pair[0] - pair[1]


def halves(row):
    return [row[:, LANES * h : LANES * h + LANES] for h in range(2)]


def put_rows(ref, at, start, rows):
    for h, half in enumerate(halves(rows)):
        ref[(*at, h, slice(8 + start, 8 + start + rows.shape[0]), slice(None))] = half


def get_rows(ref, at, start, size):
    return jnp.concatenate([ref[(*at, h, slice(8 + start, 8 + start + size), slice(None))] for h in range(2)], axis=1)


def relaxed(field, around):
    return (field + around * (1.0 / 6.0)) * (1.0 / 6.0)


def ana_edge_kernel(tiles_ref, to_low_ref, to_high_ref, low_ref, high_ref, sem):
    snaps = to_low_ref.shape[0]
    fields, layers, rows, lanes = low_ref.shape
    last = tiles_ref.shape[2] - 1
    copies = []
    for s in range(snaps):
        span = pl.ds(3 * s, 3)
        for n, (at, ref) in enumerate(((0, low_ref), (last, high_ref))):
            copies.append(pltpu.make_async_copy(tiles_ref.at[span, :, at], ref.at[span], sem.at[2 * s + n]))
    for copy in copies:
        copy.start()
    flat = (fields * layers * rows, lanes)

    def column(ref, s, c, j):
        start = (s * 3 + c) * layers * rows + j
        return jnp.concatenate(
            [ref[pl.ds(start + 8 * half, layers, stride=rows), :] for half in range(2)], axis=1
        )

    zero_row = jnp.zeros((1, 2 * lanes), jnp.float32)
    for s in range(snaps):
        for n, (side_ref, out_ref, edge, second, third, sign) in enumerate(
            ((low_ref, to_low_ref, 0, 1, 2, 1.0), (high_ref, to_high_ref, 7, 6, 5, -1.0))
        ):
            copies[2 * s + n].wait()
            ref = side_ref.reshape(*flat)
            speed = [column(ref, s, 0, j) for j in (edge, second)]
            cross = [column(ref, s, 1, j) for j in (edge, second, third)]
            deep = [column(ref, s, 2, j) for j in (edge, second)]
            beside = (sign * cross[1], sign * (cross[2] - cross[0]))
            out_ref[s, 0:16, :] = cross[0]
            for n in range(2):
                along = difference(row_pair(speed[n], zero_row, zero_row))
                out_ref[s, 16 + 16 * n : 32 + 16 * n, :] = -0.5 * (
                    along + beside[n] + difference(depth_pair(deep[n]))
                )
            out_ref[s, 48:56, :] = jnp.concatenate(
                [speed[0][0:1], speed[1][0:1], speed[0][15:16], speed[1][15:16]] + [zero_row] * 4,
                axis=0,
            )


def load_kernel(source_ref, _, along_ref, cross_ref, deep_ref, force_ref, to_low_ref, to_high_ref, sem):
    snaps, layers = force_ref.shape[:2]
    fields = (along_ref, cross_ref, deep_ref)
    copies = [
        pltpu.make_async_copy(source_ref.at[n], fields[n % 3].at[n // 3], sem.at[n]) for n in range(3 * snaps)
    ]
    for copy in copies:
        copy.start()
    for s in range(snaps):
        for copy in copies[3 * s : 3 * s + 3]:
            copy.wait()
        for i in range(layers):
            along = 0.0
            if i < layers - 1:
                along = along + along_ref[s, i + 1]
            if i > 0:
                along = along - along_ref[s, i - 1]
            cross = row_pair(cross_ref[s, i], 0.0, 0.0)
            force_ref[s, i] = -0.5 * (
                along + difference(cross) + difference(depth_pair(deep_ref[s, i]))
            )
        for out_ref, layer, second in ((to_low_ref, 0, 1), (to_high_ref, layers - 1, layers - 2)):
            out_ref[s, 0:32, :] = force_ref[s, second]
            out_ref[s, 32:64, :] = force_ref[s, layer]
            out_ref[s, 64:96, :] = along_ref[s, layer]


def fix_kernel(cross_ref, force_ref, from_low_ref, from_high_ref, to_low_ref, to_high_ref):
    layers = force_ref.shape[1]
    keep_low, keep_high = inside("ana")
    for s in range(to_low_ref.shape[0]):
        for out_ref, layer, second, pillar in ((to_low_ref, 0, 1, 48), (to_high_ref, layers - 1, layers - 2, 50)):

            def halo(side_ref, keep, row):
                return jnp.where(keep, side_ref[s, row : row + 1, :], 0.0)

            cross = cross_ref[s, layer]
            row = 16 + layer
            below = jnp.where(keep_low, from_low_ref[s, row : row + 1, :] - 0.5 * cross[0:1], 0.0)
            above = jnp.where(keep_high, from_high_ref[s, row : row + 1, :] + 0.5 * cross[31:32], 0.0)
            rows = [
                force_ref[s, layer, 0:1, :] + 0.5 * halo(from_low_ref, keep_low, layer),
                force_ref[s, layer, 31:32, :] - 0.5 * halo(from_high_ref, keep_high, layer),
                force_ref[s, second, 0:1, :] + 0.5 * halo(from_low_ref, keep_low, second),
                force_ref[s, second, 31:32, :] - 0.5 * halo(from_high_ref, keep_high, second),
                halo(from_low_ref, keep_low, pillar + 1),
                halo(from_low_ref, keep_low, pillar),
                halo(from_high_ref, keep_high, pillar),
                halo(from_high_ref, keep_high, pillar + 1),
                below,
                above,
            ]
            rows = rows + [jnp.zeros_like(below)] * (FIX_ROWS - len(rows))
            out_ref[s] = jnp.concatenate(rows, axis=0)


def sample_layers(s, parts, layers, fields, owner, weight_ref, pool_ref, out_ref, split_ref, pooled_ref, press):
    count = len(layers)
    for n, i in enumerate(layers):
        centre = get_rows(*press(i), 0, 32)
        gradient = (
            get_rows(*press(i + 1), 0, 32) - get_rows(*press(i - 1), 0, 32),
            get_rows(*press(i), 1, 32) - get_rows(*press(i), -1, 32),
            difference(depth_pair(centre)),
        )
        weight = weight_ref[32 * i : 32 * i + 32, :]
        for c in range(3):
            kept = (fields[c][s, i] - 0.5 * gradient[c]) * weight
            row = 32 * (c * count + n)
            for p in range(parts):
                piece = kept.astype(jnp.bfloat16)
                split_ref[row : row + 32, 256 * p : 256 * p + 256] = piece
                if p < parts - 1:
                    kept = kept - piece.astype(jnp.float32)
    pooled = jnp.dot(split_ref[...], pool_ref[...], preferred_element_type=jnp.float32)
    pooled_ref[0] = pooled[:, :LANES]
    pooled_ref[1] = pooled[:, LANES:]
    rows = 3 * count * 32
    flat = pooled_ref.reshape(2 * rows, LANES)
    for n, i in enumerate(layers):
        for half in range(2):
            place = owner(2 * i + half)
            for c in range(3):
                start = 32 * (c * count + n) + 16 * half
                tile = flat[pl.ds(start, 8, stride=2), :] + flat[pl.ds(start + rows + 1, 8, stride=2), :]
                out_ref[place, c, pl.ds(s, 8, stride=4), :] = tile


def inner_kernel(
    parts, owner_ref, along_ref, cross_ref, deep_ref, own_force_ref, weight_ref, pool_ref, low_ref, high_ref,
    force_ref, press_ref, out_ref, sides_ref, split_ref, pooled_ref,
):
    layers = along_ref.shape[1]
    keep_low, keep_high = inside("ana")
    brick = lax.axis_index("brick")

    def snapshot(s):
        side_ref = sides_ref.at[s]
        def halo(ref, keep, start, size=1):
            return jnp.where(keep, ref[s, start : start + size, :], 0.0)

        row_at = lax.broadcasted_iota(jnp.int32, (8, along_ref.shape[3]), 0)
        for i in range(layers):
            first, last = own_force_ref[s, i, 0:8, :], own_force_ref[s, i, 24:32, :]
            put_rows(force_ref, (s, i), 0, jnp.where(row_at == 0, first + 0.5 * halo(low_ref, keep_low, i), first))
            put_rows(force_ref, (s, i), 8, own_force_ref[s, i, 8:24, :])
            put_rows(force_ref, (s, i), 24, jnp.where(row_at == 7, last - 0.5 * halo(high_ref, keep_high, i), last))

        for side, ref, keep, row, sign in ((0, low_ref, keep_low, 0, -0.5), (1, high_ref, keep_high, 31, 0.5)):
            own_cross = jnp.concatenate([cross_ref[s, i, row : row + 1, :] for i in range(layers)], axis=0)
            own_force = jnp.concatenate([get_rows(force_ref, (s, i), row, 1) for i in range(layers)], axis=0)
            edge = ref[s, 16:32, :] + sign * own_cross
            zero_row = jnp.zeros((1, edge.shape[1]), jnp.float32)
            around = sum(row_pair(edge, zero_row, zero_row)) + ref[s, 32:48, :] + own_force
            around = around + sum(depth_pair(edge))
            side_ref[2 + side] = jnp.where(keep, edge, 0.0)
            side_ref[side] = jnp.where(keep, relaxed(edge, around), 0.0)

        for i in range(layers):
            put_rows(force_ref, (s, i), -1, side_ref[2, i : i + 1, :])
            put_rows(force_ref, (s, i), 32, side_ref[3, i : i + 1, :])
        for i in range(MARGIN - 1, layers - MARGIN + 1):
            field = get_rows(force_ref, (s, i), 0, 32)
            around = get_rows(force_ref, (s, i + 1), 0, 32) + get_rows(force_ref, (s, i - 1), 0, 32)
            around = around + (get_rows(force_ref, (s, i), 1, 32) + get_rows(force_ref, (s, i), -1, 32))
            put_rows(press_ref, (s, i), 0, relaxed(field, around + sum(depth_pair(field))))
            put_rows(press_ref, (s, i), -1, side_ref[0, i : i + 1, :])
            put_rows(press_ref, (s, i), 32, side_ref[1, i : i + 1, :])

        sample_layers(
            s, parts, list(range(MARGIN, layers - MARGIN)), (along_ref, cross_ref, deep_ref),
            lambda k: owner_ref[brick, k], weight_ref, pool_ref,
            out_ref, split_ref.at[s], pooled_ref.at[s],
            lambda i: (press_ref, (s, i)),
        )
    for s in range(along_ref.shape[0]):
        snapshot(s)


def outer_kernel(
    parts, owner_ref, along_ref, cross_ref, deep_ref, weight_ref, pool_ref, low_ref, high_ref, before_ref, after_ref,
    before_fix_ref, after_fix_ref, inner_force_ref, inner_press_ref, _, out_ref, forces_ref, presses_ref, side_forces_ref, side_presses_ref,
    split_ref, pooled_ref,
):
    layers = along_ref.shape[1]
    keep_before, keep_after = inside("brick")
    keep_low, keep_high = inside("ana")
    brick = lax.axis_index("brick")

    def snapshot(s):
        force_ref, press_ref = forces_ref.at[s], presses_ref.at[s]
        side_force_ref, side_press_ref = side_forces_ref.at[s], side_presses_ref.at[s]
        def halo(ref, keep, start, size=1):
            return jnp.where(keep, ref[s, start : start + size, :], 0.0)

        def fixed(ref, fix_ref, start, row):
            field = ref[s, start : start + 32, :]
            row_at = lax.broadcasted_iota(jnp.int32, field.shape, 0)
            field = jnp.where(row_at == 0, fix_ref[s, row : row + 1, :], field)
            return jnp.where(row_at == 31, fix_ref[s, row + 1 : row + 2, :], field)

        first, last = along_ref[s, 0], along_ref[s, layers - 1]
        edges = (
            jnp.where(keep_before, fixed(before_ref, before_fix_ref, 0, 2), 0.0),
            jnp.where(keep_before, fixed(before_ref, before_fix_ref, 32, 0) - 0.5 * first, 0.0),
            get_rows(inner_force_ref, (s, 0), 0, 32) + 0.5 * halo(before_ref, keep_before, 64, 32),
            get_rows(inner_force_ref, (s, layers - 1), 0, 32) - 0.5 * halo(after_ref, keep_after, 64, 32),
            jnp.where(keep_after, fixed(after_ref, after_fix_ref, 32, 0) + 0.5 * last, 0.0),
            jnp.where(keep_after, fixed(after_ref, after_fix_ref, 0, 2), 0.0),
        )
        for n, edge in enumerate(edges):
            put_rows(force_ref, (n,), 0, edge)

        def force(i):
            if i < 1:
                return force_ref, (i + 2,)
            if i > layers - 2:
                return force_ref, (i - layers + 4,)
            return inner_force_ref, (s, i)

        for side, ref, keep, far, near, corner, row, sign in (
            (0, low_ref, keep_low, 4, 5, 8, 0, -0.5),
            (1, high_ref, keep_high, 7, 6, 9, 31, 0.5),
        ):
            own_cross = jnp.concatenate([cross_ref[s, i, row : row + 1, :] for i in range(layers)], axis=0)
            own_force = jnp.concatenate(
                [get_rows(*force(i), row, 1) for i in range(layers)],
                axis=0,
            )
            row_at = lax.broadcasted_iota(jnp.int32, own_force.shape, 0)

            def ends(at):
                first = 0.5 * halo(before_fix_ref, keep_before, at)
                last = -0.5 * halo(after_fix_ref, keep_after, at)
                return jnp.where(row_at == 0, first, 0.0) + jnp.where(row_at == layers - 1, last, 0.0)

            edge = jnp.where(keep, ref[s, 16:32, :] + sign * own_cross + ends(near), 0.0)
            beyond = jnp.where(keep, ref[s, 32:48, :] + ends(far), 0.0)
            corner_before = jnp.where(keep_before, halo(before_fix_ref, keep, corner) - 0.5 * halo(ref, keep, 48), 0.0)
            corner_after = jnp.where(keep_after, halo(after_fix_ref, keep, corner) + 0.5 * halo(ref, keep, 50), 0.0)
            around = sum(row_pair(edge, corner_after, corner_before)) + beyond + own_force
            around = around + sum(depth_pair(edge))
            side_press_ref[side] = jnp.where(keep, relaxed(edge, around), 0.0)
            side_force_ref[side, 8:24, :] = edge
            side_force_ref[side, 7:8, :] = corner_before
            side_force_ref[side, 24:25, :] = corner_after

        low_layers, high_layers = list(range(-1, MARGIN - 1)), list(range(layers - MARGIN + 1, layers + 1))
        place = {i: n for n, i in enumerate(low_layers + high_layers)}
        for i in (-1, 0, layers - 1, layers):
            put_rows(*force(i), -1, side_force_ref[0, 8 + i : 9 + i, :])
            put_rows(*force(i), 32, side_force_ref[1, 8 + i : 9 + i, :])
        for i in place:
            field = get_rows(*force(i), 0, 32)
            around = get_rows(*force(i + 1), 0, 32) + get_rows(*force(i - 1), 0, 32)
            around = around + (get_rows(*force(i), 1, 32) + get_rows(*force(i), -1, 32))
            press = relaxed(field, around + sum(depth_pair(field)))
            if i == -1:
                press = jnp.where(keep_before, press, 0.0)
            if i == layers:
                press = jnp.where(keep_after, press, 0.0)
            put_rows(press_ref, (place[i],), 0, press)
            if 0 <= i < layers:
                put_rows(press_ref, (place[i],), -1, side_press_ref[0, i : i + 1, :])
                put_rows(press_ref, (place[i],), 32, side_press_ref[1, i : i + 1, :])

        sample_layers(
            s, parts, list(range(MARGIN)) + list(range(layers - MARGIN, layers)), (along_ref, cross_ref, deep_ref),
            lambda k: owner_ref[brick, k], weight_ref, pool_ref, out_ref, split_ref.at[s], pooled_ref.at[s],
            lambda i: (press_ref, (place[i],)) if i in place else (inner_press_ref, (s, i)),
        )
    for s in range(along_ref.shape[0]):
        snapshot(s)


def weight_kernel(parts, index_ref, out_ref, pool_ref, wide_ref):
    pool_ref[...] = pooling(parts)
    rows = index_ref.shape[0]
    at = lax.broadcasted_iota(jnp.int32, (rows, LANES), 0) * LANES + lax.broadcasted_iota(jnp.int32, (rows, LANES), 1)
    offset = (index_ref[...] - 4 * at).astype(jnp.float32).astype(jnp.bfloat16)
    source = lax.broadcasted_iota(jnp.int32, (LANES, 512), 0)
    target = lax.broadcasted_iota(jnp.int32, (LANES, 512), 1)
    expand = jnp.where(target // 4 == source, 1.0, 0.0).astype(jnp.bfloat16)
    wide = jnp.dot(offset, expand, preferred_element_type=jnp.float32)
    lane_at = lax.broadcasted_iota(jnp.int32, wide.shape, 1)
    hit = jnp.where(wide == (lane_at % 4).astype(jnp.float32), 1.0, 0.0)
    for half in range(2):
        for kt in range(2):
            wide_ref[kt, pl.ds(half, rows, stride=2), :] = hit[:, 256 * half + 128 * kt : 256 * half + 128 * kt + 128]
    for kt in range(2):
        out_ref[:, 128 * kt : 128 * kt + 128] = wide_ref[kt]


def pooling(parts):
    source = lax.broadcasted_iota(jnp.int32, (256 * parts, 256), 0) % 256
    target = lax.broadcasted_iota(jnp.int32, (256 * parts, 256), 1)
    low = (target < 64) & (source // 4 == target)
    high = (target >= 192) & (source // 4 == target - 192)
    return jnp.where(low | high, 1.0, 0.0).astype(jnp.bfloat16)


def exchange(to_before, to_after, axis):
    devices = lax.axis_size(axis)
    up = [(i, (i + 1) % devices) for i in range(devices)]
    down = [(j, i) for i, j in up]
    return lax.ppermute(to_after, axis, up), lax.ppermute(to_before, axis, down)


def grid_kernel(kernel, name, cost, **kwargs):
    flops, data = cost
    return pl.pallas_call(
        kernel,
        compiler_params=pltpu.CompilerParams(vmem_limit_bytes=VMEM_LIMIT),
        cost_estimate=pl.CostEstimate(flops=flops, bytes_accessed=data, transcendentals=0),
        name=name,
        **kwargs,
    )


def front(provisional, sample_index, owner_table):
    snaps, comps, layers, columns, depth = provisional.shape
    bricks = lax.axis_size("brick")
    smem = pl.BlockSpec(memory_space=pltpu.SMEM)
    vmem = pl.BlockSpec(memory_space=pltpu.VMEM)
    samples = layers * columns * depth // 4
    source = provisional.reshape(snaps * comps, layers, columns, depth)
    f32 = lambda *shape: jax.ShapeDtypeStruct(shape, jnp.float32)
    scratch = lambda *shape: pltpu.VMEM(shape, jnp.float32)

    tiles = source.reshape(snaps * comps, layers, columns // 8, 8, 2, LANES)
    tiles = tiles.transpose(0, 1, 2, 4, 3, 5).reshape(snaps * comps, layers, columns // 8, 16, LANES)
    to_low, to_high = grid_kernel(
        ana_edge_kernel,
        "ana_edges",
        (10**6, 4 * 10**6),
        in_specs=[pl.BlockSpec(memory_space=pltpu.HBM)],
        out_specs=[vmem] * 2,
        out_shape=[f32(snaps, ANA_ROWS, depth)] * 2,
        scratch_shapes=[scratch(snaps * comps, layers, 16, LANES)] * 2 + [pltpu.SemaphoreType.DMA((2 * snaps,))],
    )(pltpu.with_memory_space_constraint(tiles, pltpu.HBM))
    from_low, from_high = exchange(to_low, to_high, "ana")

    weight, pool = grid_kernel(
        functools.partial(weight_kernel, POOL_PARTS),
        "weights",
        (10**6, 10**6),
        in_specs=[vmem],
        out_specs=[vmem] * 2,
        out_shape=[f32(layers * columns, depth), jax.ShapeDtypeStruct((256 * POOL_PARTS, 256), jnp.bfloat16)],
        scratch_shapes=[scratch(2, layers * columns, LANES)],
    )(sample_index.reshape(samples // LANES, LANES))

    *fields, own_force, to_before, to_after = grid_kernel(
        load_kernel,
        "load",
        (10**8, 6 * 10**6),
        in_specs=[pl.BlockSpec(memory_space=pltpu.HBM), pl.BlockSpec(memory_space=pl.ANY)],
        out_specs=[vmem] * 6,
        out_shape=[f32(snaps, layers, columns, depth)] * 4 + [f32(snaps, BULK_ROWS, depth)] * 2,
        scratch_shapes=[pltpu.SemaphoreType.DMA((snaps * comps,))],
    )(pltpu.with_memory_space_constraint(source, pltpu.HBM), to_low)
    from_before, from_after = exchange(to_before, to_after, "brick")

    to_before, to_after = grid_kernel(
        fix_kernel,
        "fix",
        (10**5, 10**6),
        in_specs=[vmem] * 4,
        out_specs=[vmem] * 2,
        out_shape=[f32(snaps, FIX_ROWS, depth)] * 2,
    )(fields[1], own_force, from_low, from_high)
    before_fix, after_fix = exchange(to_before, to_after, "brick")

    split_shape = lambda count: pltpu.VMEM((snaps, 3 * 32 * count, 256 * POOL_PARTS), jnp.bfloat16)
    force, press, outgoing = grid_kernel(
        functools.partial(inner_kernel, POOL_PARTS),
        "inner_layers",
        (4 * 10**9, 2 * 10**7),
        in_specs=[smem] + [vmem] * 8,
        out_specs=[vmem] * 3,
        out_shape=[f32(snaps, layers, 2, PADDED, LANES)] * 2 + [f32(bricks, comps, 32, LANES)],
        scratch_shapes=[
            scratch(snaps, 4, layers, depth),
            split_shape(layers - 2 * MARGIN),
            scratch(snaps, 2, 3 * 32 * (layers - 2 * MARGIN), LANES),
        ],
    )(owner_table, *fields, own_force, weight, pool, from_low, from_high)
    return grid_kernel(
        functools.partial(outer_kernel, POOL_PARTS),
        "outer_layers",
        (3 * 10**9, 10**7),
        in_specs=[smem] + [vmem] * 14,
        out_specs=vmem,
        out_shape=f32(bricks, comps, 32, LANES),
        scratch_shapes=[
            scratch(snaps, 6, 2, PADDED, LANES),
            scratch(snaps, 2 * MARGIN, 2, PADDED, LANES),
            scratch(snaps, 2, 32, depth),
            scratch(snaps, 2, layers, depth),
            split_shape(2 * MARGIN),
            scratch(snaps, 2, 3 * 32 * 2 * MARGIN, LANES),
        ],
        input_output_aliases={14: 0},
    )(owner_table, *fields, weight, pool, from_low, from_high, from_before, from_after, before_fix, after_fix, force, press, outgoing)


def per_device(provisional, sample_index, owner_table, weighted_basis):
    snaps = provisional.shape[0]
    rank_count = weighted_basis.shape[0]
    devices = lax.axis_size("brick") * lax.axis_size("ana")
    total_rows = 3.0 * sample_index.shape[2] * devices
    outgoing = front(provisional, sample_index, owner_table)
    arrived = lax.all_to_all(outgoing, "brick", split_axis=0, concat_axis=0, tiled=True)
    basis = jnp.transpose(weighted_basis, (1, 0, 2))
    new_basis, core = tail(basis, arrived, WIDTH, total_rows, devices)
    count = rank_count + snaps
    return (jnp.transpose(new_basis, (1, 0, 2)), core[:count, :count])


def solution(mesh):
    placed = (
        P(None, None, "brick", "ana", None),
        P("brick", "ana", None),
        P(),
        P(None, None, ("brick", "ana")),
    )
    return jax.shard_map(
        per_device,
        mesh=mesh,
        in_specs=placed,
        out_specs=(P(None, None, ("brick", "ana")), P()),
        check_vma=False,
    )
```
